512 devices in a mesh: row: 16 (over z_lo, x), col: 8 (over y), vir: 4 (over z_hi, core).
Axes of the slice: x: 4, y: 8, z: 8 (z_hi: 2, z_lo: 4; z = z_hi * 4 + z_lo), core: 2. Of those that a mesh axis runs over, the one named last changes fastest.
Arguments:
- amplitudes: bfloat16 [8, 16, 1, 8, 16, 3, 1792], P(None, 'row', None, 'col'), may hold values from -6 to 6
- integrals: bfloat16 [64, 64, 3, 1792], P('vir', 'row', None, 'col'), may hold values from -0.25 to 0.25
- hole_integrals: bfloat16 [128, 1, 8, 16, 3, 64], P(None, None, 'col'), may hold values from -0.3125 to 0.3125
- irreps: int32 [112], replicated, may hold values from 0 to 7
- occ_energy: float32 [128], replicated, may hold values from -2 to -0.5
- vir_energy: float32 [64], replicated, may hold values from 0.5 to 3
Outputs:
- increment: bfloat16 [8, 16, 1, 8, 16, 64, 64], P(None, 'row', None, 'col', None, 'vir')
The draws below stay inside these ranges and needn't reach their ends.
All inputs are finite; a program needn't handle non-finite values.
Results may differ from the reference program's by a relative error of at most 0.001.
Values may be sent and summed in bfloat16 or wider, within the bound.
A program may use at most 128 MiB of HBM per device.

```python
import jax
import jax.numpy as jnp
from jax import lax

NO = 128
NV = 1792
SA = 64
CW = 3
VBLK = 16
N_ROW = 16
N_COL = 8


def plant(drawn, key, least, largest):
    longest = drawn.shape.index(max(drawn.shape))
    spots = []
    for shift in (0, 1):
        where = [jax.random.randint(jax.random.fold_in(key, axis), (), 0, length) for axis, length in enumerate(drawn.shape)]
        where[longest] = (where[longest] + shift) % drawn.shape[longest]
        spots.append(tuple(where))
    return drawn.at[spots[0]].set(least).at[spots[1]].set(largest)


def level_of(stream_key, shape, shards, least, largest):
    gain, own = 1.0, jax.random.fold_in(stream_key, 6)
    for position, blocks in shards:
        steps = jnp.exp(jax.random.uniform(jax.random.fold_in(own, position), (blocks,), jnp.float32, least / len(shards), largest / len(shards)))
        gain = gain * jnp.repeat(steps, shape[position] // blocks).reshape([-1 if axis == position else 1 for axis in range(len(shape))])
    return gain


def noise(stream_key, extent, spread, bound, pieces=(), held_as=jnp.bfloat16):
    loudness = level_of(stream_key, extent, pieces, -0.22, 0.18) if pieces else 1.0
    values = jax.random.normal(stream_key, extent, jnp.float32) * spread * loudness
    return jnp.minimum(jnp.maximum(values, -bound), bound).astype(held_as)


def setup_inputs(seed: int = 0) -> dict:
    keys = jax.random.split(jax.random.key(seed), 7)
    amplitudes = noise(keys[0], (NO // N_ROW, N_ROW, NO // (N_ROW * N_COL), N_COL, N_ROW, CW, NV), 1.0, 6.0, ((1, 16), (3, 8)))
    integrals = noise(keys[1], (SA, SA, CW, NV), (CW * NV // 8) ** -0.5, 0.25, ((0, 4), (1, 16), (3, 8)))
    hole_integrals = noise(keys[2], (NO, NO // (N_ROW * N_COL), N_COL, N_ROW, CW, SA), (NO * CW) ** -0.5, 0.3125, ((2, 8),))
    irreps = plant(jax.random.randint(keys[3], (NV // VBLK,), 0, 8), jax.random.fold_in(keys[3], 1), 0, 7).astype(jnp.int32)
    occ_energy = jnp.clip(jax.random.uniform(keys[4], (NO,), jnp.float32, -2.0, -0.5), -2.0, -0.5)
    vir_energy = jnp.clip(jax.random.uniform(keys[5], (SA,), jnp.float32, 0.5, 3.0), 0.5, 3.0)
    return dict(amplitudes=amplitudes, integrals=integrals, hole_integrals=hole_integrals, irreps=irreps, occ_energy=occ_energy, vir_energy=vir_energy)


def reference(amplitudes, integrals, hole_integrals, irreps, occ_energy, vir_energy):
    amps = amplitudes.reshape(NO, NO, CW, NV)
    wmat = hole_integrals.reshape(NO, NO, CW, SA).astype(jnp.float32)
    labels = jnp.repeat(irreps, VBLK)
    left = jnp.bitwise_xor(labels[:SA][:, None], labels[:SA][None, :])
    right = jnp.bitwise_xor(labels[:CW][:, None], labels[None, :])
    keep = left[:, :, None, None] == right[None, None, :, :]
    masked = jnp.where(keep, integrals, jnp.zeros_like(integrals)).astype(jnp.float32)
    slab_amps = amps[:, :, :, :SA]

    def per_row(index):
        first = lax.dynamic_index_in_dim(amps, index, 0, keepdims=False).astype(jnp.float32)
        ladder = lax.dot_general(first, masked, (((1, 2), (2, 3)), ((), ())), preferred_element_type=jnp.float32)
        along = lax.dynamic_index_in_dim(slab_amps, index, 0, keepdims=False).astype(jnp.float32)
        crossed = -lax.dot_general(along, wmat, (((0, 1), (0, 2)), ((), ())), preferred_element_type=jnp.float32)
        return ladder + jnp.transpose(crossed, (1, 0, 2))

    mixed = lax.map(per_row, jnp.arange(NO, dtype=jnp.int32))
    summed = mixed + jnp.transpose(mixed, (1, 0, 3, 2))
    denom = (occ_energy[:, None, None, None] + occ_energy[None, :, None, None]
             - vir_energy[None, None, :, None] - vir_energy[None, None, None, :])
    result = (summed / denom).astype(jnp.bfloat16)
    return result.reshape(NO // N_ROW, N_ROW, NO // (N_ROW * N_COL), N_COL, N_ROW, SA, SA)
```

```python
import jax
import jax.numpy as jnp
from jax import lax
from jax.experimental import pallas as pl
from jax.experimental.pallas import tpu as pltpu
from jax.sharding import PartitionSpec as P

NO = 128
NV = 1792
SA = 64
CW = 3
VBLK = 16
KK = CW * NV
NX, NY, NZL = 4, 8, 4
DW = NV // NY
PIECE = CW * 256
MESH = pl.DeviceIdType.MESH
NT = (((1,), (1,)), ((), ()))
NN = (((1,), (0,)), ((), ()))


def dev(x, y, z, k):
    return (lax.rem(z, NZL) * NX + x, y, lax.div(z, NZL) * 2 + k)


def dot(a, b, dims=NN):
    return lax.dot_general(a, b, dims, preferred_element_type=jnp.float32)


def iota2(shape):
    return (
        lax.broadcasted_iota(jnp.int32, shape, 0),
        lax.broadcasted_iota(jnp.int32, shape, 1),
    )


def ones_where(cond):
    return jnp.where(cond, 1.0, 0.0).astype(jnp.bfloat16)


def kernel(
    t_ref, v_ref, a_ref, w_ref, ps_ref, ea_ref, eb_ref, out_ref,
    t_all, v_stage, v_all, a_all, acc, lhs_hi, lhs_lo, place, mail, d_all, rec, swap, sbuf, order,
    t_own_sem, ty_send, ty_recv, tf_send, tf_recv, sib_send, sib_recv,
    vy_send, vy_recv, vx_send, vx_recv, vf_send, vf_recv,
    a_send, a_recv, d_send, d_recv, m_send, m_recv,
):
    r = lax.axis_index("row")
    y = lax.axis_index("col")
    v = lax.axis_index("vir")
    x, zl = lax.rem(r, NX), lax.div(r, NX)
    zh, k = lax.div(v, 2), lax.rem(v, 2)
    z = zh * NZL + zl
    xs = (lax.rem(x + 1, NX), lax.rem(x + NX - 1, NX))
    ys = (lax.rem(y + 1, NY), lax.rem(y + NY - 1, NY))
    zs = (lax.rem(z + 1, 8), lax.rem(z + 7, 8))
    is_self = zl == v

    own = pltpu.make_async_copy(t_ref, t_all.at[pl.ds(0, 128)], t_own_sem)
    own.start()

    barrier = pltpu.get_barrier_semaphore()

    def greet(where):
        pl.semaphore_signal(barrier, inc=1, device_id=where, device_id_type=MESH)

    for d in range(2):
        greet(dev(x, ys[d], z, k))
        greet(dev(xs[d], y, z, k))
        greet(dev(x, y, zs[d], k))
    greet(dev(x, y, z, 1 - k))

    def greet_slab(n, carry):
        nz, ny = lax.div(n, NY), lax.rem(n, NY)
        greet(dev(x, lax.rem(y + ny, NY), zh * NZL + lax.rem(zl + nz, NZL), k))
        return carry

    lax.fori_loop(1, 32, greet_slab, 0)

    def greet_mail(n, carry):
        sx, sy, sv = lax.rem(n, 4), lax.rem(lax.div(n, 4), 8), lax.div(n, 32)
        row = v * NX + sx
        mine = jnp.logical_and(jnp.logical_and(row == r, sy == y), sv == v)

        @pl.when(jnp.logical_not(mine))
        def _():
            greet((row, sy, sv))

        return carry

    lax.fori_loop(0, 128, greet_mail, 0)
    pl.semaphore_wait(barrier, 7 + 31 + 128 - jnp.where(is_self, 1, 0))
    own.wait()

    def remote(src, dst, send, recv, where):
        return pltpu.make_async_remote_copy(
            src_ref=src, dst_ref=dst, send_sem=send, recv_sem=recv, device_id=where, device_id_type=MESH
        )

    sends = []

    def go(copy):
        copy.start()
        sends.append(copy)

    def t_rows(block, h):
        return pl.ds(pl.multiple_of(block * 128 + k * 64 + h * 32, 32), 32)

    t_block = (3, 1)

    def t_copy(d, h):
        return remote(
            t_all.at[t_rows(0, h)], t_all.at[t_rows(t_block[d], h)], ty_send.at[d, h], ty_recv.at[d, h],
            dev(x, y, zs[d], k),
        )

    def t_forward(d):
        h = d
        return remote(
            t_all.at[t_rows(t_block[d], h)], t_all.at[t_rows(2, h)], tf_send.at[d], tf_recv.at[d],
            dev(x, y, zs[d], k),
        )

    def t_sibling(block, h):
        rows = t_rows(block, h)
        return remote(
            t_all.at[rows], t_all.at[rows], sib_send.at[block - 1, h], sib_recv.at[block - 1, h],
            dev(x, y, z, 1 - k),
        )

    def vy_copy(d, s, h):
        slot = lax.rem(y + (NY - s if d == 0 else s), NY)
        rows = pl.ds(h * 32, 32)
        return remote(
            v_stage.at[slot, rows], v_stage.at[slot, rows], vy_send.at[d, s, h], vy_recv.at[d, s, h],
            dev(x, ys[d], z, k),
        )

    def v_rows(slot, h):
        return pl.ds(pl.multiple_of(slot * 64 + h * 32, 32), 32)

    def vx_copy(d, h):
        rows = v_rows(x, h)
        return remote(
            v_all.at[rows], v_all.at[rows], vx_send.at[d, h], vx_recv.at[d, h], dev(xs[d], y, z, k)
        )

    def vx_forward(d):
        rows = v_rows(xs[1 - d], d)
        return remote(
            v_all.at[rows], v_all.at[rows], vf_send.at[d], vf_recv.at[d], dev(xs[d], y, z, k)
        )

    v_stage[y] = v_ref[...]
    a_all[y] = a_ref[...]
    for h in range(2):
        go(vy_copy(0, 0, h))
        go(vy_copy(1, 0, h))
    go(t_copy(0, 0))
    go(t_copy(1, 1))
    go(t_copy(0, 1))
    go(t_copy(1, 0))

    def slab_copy(n):
        nz, ny = lax.div(n, NY), lax.rem(n, NY)
        block = lax.rem(NZL - nz, NZL)
        return remote(
            a_ref, a_all.at[block * NY + y], a_send, a_recv,
            dev(x, lax.rem(y + ny, NY), zh * NZL + lax.rem(zl + nz, NZL), k),
        )

    def send_slab(n, carry):
        slab_copy(n).start()
        return carry

    lax.fori_loop(1, 32, send_slab, 0)

    for s in range(4):
        for h in range(2):
            vy_copy(0, s, h).wait_recv()
            if s < 3:
                go(vy_copy(0, s + 1, h))
                vy_copy(1, s, h).wait_recv()
            if s < 2:
                go(vy_copy(1, s + 1, h))
            if s == 3:
                rows = pl.ds(h * 32, 32)
                for c in range(CW):
                    for half in range(2):
                        joined = jnp.concatenate(
                            [v_stage[half * 4 + q, rows, c * 256 : c * 256 + DW] for q in range(4)], axis=1
                        )
                        v_all[v_rows(x, h), c * NV + half * 896 : c * NV + (half + 1) * 896] = joined
                go(vx_copy(0, h))
                go(vx_copy(1, h))

    m, n = iota2((2048, 256))
    place[...] = ones_where(jnp.logical_and(m >> 7 == n >> 4, (m & 15) == (n & 15)))
    m, n = iota2((256, 256))
    swap[...] = ones_where(jnp.logical_and(m >> 4 == (n & 15), (m & 15) == n >> 4))

    def build_order(i, carry):
        m, n = iota2((256, 1024))
        hit = jnp.logical_and(m >> 4 == n >> 6, (m & 15) == (n & 15))
        hit = jnp.logical_and(hit, ((n >> 4) & 3) == i)
        order[pl.ds(pl.multiple_of(i * 256, 256), 256), :] = ones_where(hit)
        return carry

    lax.fori_loop(0, 4, build_order, 0)

    t_copy(0, 0).wait_recv()
    go(t_forward(0))
    go(t_sibling(3, 0))
    t_copy(1, 1).wait_recv()
    go(t_forward(1))
    go(t_sibling(1, 1))

    pltpu.make_async_copy(a_all.at[pl.ds(0, 31)], a_all.at[pl.ds(0, 31)], a_recv).wait()
    m, n = iota2((32, 128))
    keep = m >> 2 == n >> 4

    def crossed(block, carry):
        slab = a_all[pl.ds(block * NY, NY)].reshape(NO * CW, 128)
        zr = dot(w_ref[...], slab)
        for b in range(16):
            for q in range(4):
                part = zr[b * 32 + q * 8 : b * 32 + q * 8 + 8, :]
                wide = jnp.where(keep, jnp.concatenate([part] * 4, axis=0), 0.0)
                hi = wide.astype(jnp.bfloat16)
                lhs_hi[q * 32 : q * 32 + 32, b * 128 : b * 128 + 128] = hi
                lhs_lo[q * 32 : q * 32 + 32, b * 128 : b * 128 + 128] = (
                    wide - hi.astype(jnp.float32)
                ).astype(jnp.bfloat16)
        rows = pl.ds(pl.multiple_of(block * 128, 128), 128)
        acc[rows, :] = dot(lhs_hi[...], place[...]) + dot(lhs_lo[...], place[...])
        return carry

    lax.fori_loop(0, 4, crossed, 0)

    vx_copy(0, 0).wait_recv()
    go(vx_forward(0))
    t_copy(0, 1).wait_recv()
    go(t_sibling(3, 1))
    t_copy(1, 0).wait_recv()
    go(t_sibling(1, 0))
    vx_copy(1, 1).wait_recv()
    go(vx_forward(1))
    vx_copy(0, 1).wait_recv()
    vx_copy(1, 0).wait_recv()
    for d in range(2):
        t_forward(d).wait_recv()
        go(t_sibling(2, d))
    for d in range(2):
        vx_forward(d).wait_recv()
    for block in (3, 1, 2):
        for h in range(2):
            t_sibling(block, h).wait_recv()

    def ladder(i, carry):
        ks = pl.ds(pl.multiple_of(i * 768, 768), 768)
        acc[...] += dot(t_all[:, ks], v_all[:, ks], NT)
        return carry

    lax.fori_loop(0, KK // 768, ladder, 0)

    for block in range(1, 4):
        there = zh * NZL + lax.rem(zl + block, NZL)
        copy = remote(
            acc.at[pl.ds(block * 128, 128)], d_all.at[zl], d_send.at[block - 1], d_recv, dev(x, y, there, k)
        )
        go(copy)
    d_all[zl] = acc[pl.ds(0, 128), :]

    for block in range(4):
        for h in range(2):
            mail[:, block * 2 + h, :] = acc[block * 128 : block * 128 + 128, h * 128 : h * 128 + 128]
    here = v * 32 + y * 4 + x

    def send_mail(n, carry):
        pj = lax.rem(r + n, 16)
        qi = lax.rem(y + lax.div(n, 16), NY)
        tile = lax.div(pj, 4) * 32 + qi * 4 + lax.rem(pj, 4)
        mine = jnp.logical_and(is_self, n == 0)

        @pl.when(mine)
        def _():
            pltpu.make_async_copy(mail.at[tile], rec.at[here], m_recv).start()

        @pl.when(jnp.logical_not(mine))
        def _():
            remote(mail.at[tile], rec.at[here], m_send, m_recv, (pj, qi, zl)).start()

        return carry

    lax.fori_loop(0, 128, send_mail, 0)

    pltpu.make_async_copy(d_all.at[pl.ds(0, 3)], d_all.at[pl.ds(0, 3)], d_recv).wait()
    pltpu.make_async_copy(rec, rec, m_recv).wait()

    for vb in range(4):
        part = d_all[vb]
        hi = part.astype(jnp.bfloat16)
        rest = part - hi.astype(jnp.float32)
        mid = rest.astype(jnp.bfloat16)
        low = (rest - mid.astype(jnp.float32)).astype(jnp.bfloat16)
        d_all[vb] = dot(hi, swap[...]) + (dot(mid, swap[...]) + dot(low, swap[...]))
    for block in range(4):
        zj = lax.rem(v + block, 4)
        rows = pl.ds(pl.multiple_of(zj * 32, 32), 32)
        pair = ps_ref[rows, :]
        for vb in range(4):
            mirrored = jnp.concatenate(
                [rec[vb * 32 : vb * 32 + 32, block * 2 + h, :] for h in range(2)], axis=1
            )
            denom = (pair - ea_ref[...]) - eb_ref[vb : vb + 1, :]
            res = (d_all[vb, rows, :] + mirrored) / denom
            sbuf[rows, vb * 256 : vb * 256 + 256] = res.astype(jnp.bfloat16)
    out_ref[...] = dot(sbuf[...], order[...]).astype(jnp.bfloat16)

    for copy in sends:
        copy.wait_send()
    pltpu.make_async_copy(a_all.at[pl.ds(0, 31)], a_all.at[pl.ds(0, 31)], a_send).wait()

    @pl.when(is_self)
    def _():
        pltpu.make_async_copy(mail.at[pl.ds(0, 127)], mail.at[pl.ds(0, 127)], m_send).wait()

    @pl.when(jnp.logical_not(is_self))
    def _():
        pltpu.make_async_copy(mail, mail, m_send).wait()


def call(t, vv, a, w, ps, ea, eb):
    bf, f32 = jnp.bfloat16, jnp.float32
    vm = pl.BlockSpec(memory_space=pltpu.VMEM)
    dma = pltpu.SemaphoreType.DMA
    return pl.pallas_call(
        kernel,
        out_shape=jax.ShapeDtypeStruct((NO, 1024), bf),
        in_specs=[pl.BlockSpec(memory_space=pl.ANY)] + [vm] * 6,
        out_specs=vm,
        scratch_shapes=[
            pltpu.VMEM((512, KK), bf),
            pltpu.VMEM((NY, 64, PIECE), bf),
            pltpu.VMEM((256, KK), bf),
            pltpu.VMEM((32, 48, 128), bf),
            pltpu.VMEM((512, 256), f32),
            pltpu.VMEM((128, 2048), bf),
            pltpu.VMEM((128, 2048), bf),
            pltpu.VMEM((2048, 256), bf),
            pltpu.VMEM((128, 8, 128), f32),
            pltpu.VMEM((4, 128, 256), f32),
            pltpu.VMEM((128, 8, 128), f32),
            pltpu.VMEM((256, 256), bf),
            pltpu.VMEM((128, 1024), bf),
            pltpu.VMEM((1024, 1024), bf),
            dma,
            dma((2, 2)), dma((2, 2)), dma((2,)), dma((2,)), dma((3, 2)), dma((3, 2)),
            dma((2, 4, 2)), dma((2, 4, 2)), dma((2, 2)), dma((2, 2)), dma((2,)), dma((2,)),
            dma, dma, dma((3,)), dma, dma, dma,
        ],
        compiler_params=pltpu.CompilerParams(
            collective_id=0, has_side_effects=True, vmem_limit_bytes=48 * 1024 * 1024
        ),
        cost_estimate=pl.CostEstimate(flops=2 * 512 * 256 * KK, bytes_accessed=20_000_000, transcendentals=0),
    )(t, vv, a, w, ps, ea, eb)


def local(amplitudes, integrals, hole_integrals, irreps, occ_energy, vir_energy):
    r = lax.axis_index("row")
    y = lax.axis_index("col")
    v = lax.axis_index("vir")
    zl = lax.div(r, NX)
    amps = amplitudes.reshape(8, 4, 4, CW, NV)
    t = jnp.transpose(amps, (1, 0, 2, 3, 4)).reshape(NO, KK)
    labels = jnp.repeat(irreps, VBLK)
    lab_a = lax.dynamic_slice_in_dim(labels, v * 16, 16)
    lab_b = lax.dynamic_slice_in_dim(labels, r * 4, 4)
    lab_d = lax.dynamic_slice_in_dim(labels, y * DW, DW)
    left = jnp.bitwise_xor(lab_a[:, None], lab_b[None, :])
    right = jnp.bitwise_xor(labels[:CW][:, None], lab_d[None, :])
    keep = left[:, :, None, None] == right[None, None, :, :]
    masked = jnp.where(keep, integrals, jnp.zeros_like(integrals))
    masked = jnp.transpose(masked, (1, 0, 2, 3)).reshape(64, CW, DW)
    vv = jnp.pad(masked, ((0, 0), (0, 0), (0, 256 - DW))).reshape(64, PIECE)
    slab = lax.dynamic_slice_in_dim(amplitudes, v * 16, 16, 6).reshape(8, 16, CW, 16)
    a = jnp.transpose(slab, (1, 2, 0, 3)).reshape(48, 128)
    hole = lax.dynamic_slice_in_dim(hole_integrals, zl * 16, 16, 5).reshape(NO, 4, 1, 4, CW, 16)
    hole = jnp.broadcast_to(hole, (NO, 4, 2, 4, CW, 16))
    w = -jnp.transpose(hole, (5, 1, 2, 3, 0, 4)).reshape(512, NO * CW)
    energy_i = lax.dynamic_slice_in_dim(occ_energy.reshape(8, 16), r, 1, 1).reshape(1, 8, 1)
    energy_j = lax.dynamic_slice_in_dim(occ_energy.reshape(8, 16), y, 1, 0).reshape(4, 1, 4)
    ps = (energy_i + energy_j).reshape(NO, 1)
    energy_a = lax.dynamic_slice_in_dim(vir_energy, v * 16, 16)
    ea = jnp.broadcast_to(energy_a[:, None], (16, 16)).reshape(1, 256)
    eb = jnp.broadcast_to(vir_energy.reshape(4, 1, 16), (4, 16, 16)).reshape(4, 256)
    out = call(t, vv, a, w, ps, ea, eb)
    out = jnp.transpose(out.reshape(4, 8, 4, 16, SA), (1, 0, 2, 3, 4))
    return out.reshape(8, 1, 1, 1, 16, 16, SA)


def solution(mesh):
    in_specs = (
        P(None, "row", None, "col", None, None, None),
        P("vir", "row", None, "col"),
        P(None, None, "col", None, None, None),
        P(),
        P(),
        P(),
    )
    out_specs = P(None, "row", None, "col", None, "vir", None)
    return jax.shard_map(local, mesh=mesh, in_specs=in_specs, out_specs=out_specs, check_vma=False)
```

```python
import jax
import jax.numpy as jnp
from jax import lax
from jax.experimental import pallas as pl
from jax.experimental.pallas import tpu as pltpu
from jax.sharding import PartitionSpec as P

NO = 128
NV = 1792
SA = 64
CW = 3
VBLK = 16
KK = CW * NV
NX, NY, NZ, NZL = 4, 8, 8, 4
DW = NV // NY
PIECE = CW * 256
MESH = pl.DeviceIdType.MESH
NT = (((1,), (1,)), ((), ()))
NN = (((1,), (0,)), ((), ()))

WORK = [
    (0, 1), (1, 0), (0, 0), (1, 1), (2, 1), (1, 2), (0, 3), (3, 0),
    (2, 0), (0, 2), (1, 3), (3, 1), (2, 2), (3, 3), (2, 3), (3, 2),
]
PLACE_OF = [WORK.index((a, b)) for a in range(4) for b in range(4)]


def pick(index, table):
    value = jnp.int32(table[0])
    for n in range(1, len(table)):
        value = jnp.where(index == n, jnp.int32(table[n]), value)
    return value


def dev(x, y, z, k):
    return (lax.rem(z, NZL) * NX + x, y, lax.div(z, NZL) * 2 + k)


def dot(a, b, dims=NN):
    return lax.dot_general(a, b, dims, preferred_element_type=jnp.float32)


def remote(src, dst, send, recv, where):
    return pltpu.make_async_remote_copy(
        src_ref=src, dst_ref=dst, send_sem=send, recv_sem=recv, device_id=where, device_id_type=MESH
    )


def kernel(
    t_ref, v_ref, w_ref, irreps, occ, vir, out_ref,
    t_all, s0, s1, v_all, a_mat, zs, acc, own_x, order, swap, pull, a_own, v_own, w_own, denom, mail, rec, sbuf, d_all,
    ssem, rsem, load_sem, a_send, a_recv, m_send, m_recv, d_recv,
):
    r = lax.axis_index("row")
    y = lax.axis_index("col")
    v = lax.axis_index("vir")
    x, zl = lax.rem(r, NX), lax.div(r, NX)
    zh, k = lax.div(v, 2), lax.rem(v, 2)
    z = zh * NZL + zl
    xs = (lax.rem(x + 1, NX), lax.rem(x + NX - 1, NX))
    ys = (lax.rem(y + 1, NY), lax.rem(y + NY - 1, NY))
    zn = (lax.rem(z + 1, NZ), lax.rem(z + NZ - 1, NZ))
    blk_a = pick(z * 2 + k, [w[0] for w in WORK])
    blk_b = pick(z * 2 + k, [w[1] for w in WORK])
    diag = blk_a == blk_b
    own = blk_a == v
    twin = jnp.where(diag, k, 1 - k)

    t_loads = [
        pltpu.make_async_copy(
            t_ref.at[:, c], t_all.at[pl.ds(0, 8), :, pl.ds(c * NV, NV)], load_sem.at[c]
        )
        for c in range(CW)
    ]
    w_load = pltpu.make_async_copy(w_ref, w_own, load_sem.at[3])
    for load in t_loads:
        load.start()
    w_load.start()

    barrier = pltpu.get_barrier_semaphore()

    def greet(where):
        pl.semaphore_signal(barrier, inc=1, device_id=where, device_id_type=MESH)

    for n in range(1, NX):
        greet(dev(lax.rem(x + n, NX), y, z, k))

    def greet_y(n, carry):
        greet(dev(x, lax.rem(y + n, NY), z, k))
        return carry

    lax.fori_loop(1, NY, greet_y, 0)

    def greet_z(n, carry):
        other = lax.rem(z * 2 + k + n, 16)
        greet(dev(x, y, lax.div(other, 2), lax.rem(other, 2)))
        return carry

    lax.fori_loop(1, 16, greet_z, 0)
    first = jnp.where(diag, 1, 0)

    def partner(n):
        return (lax.rem(x + lax.rem(n, NX), NX), lax.rem(y + lax.div(n, NX), NY))

    def greet_mail(n, carry):
        px, py = partner(n)
        greet(dev(px, py, z, twin))
        return carry

    lax.fori_loop(first, 32, greet_mail, 0)
    label = jnp.bitwise_xor(jnp.bitwise_xor(irreps[v], irreps[zl]), irreps[0])
    lane = lax.broadcasted_iota(jnp.int32, (8, PIECE), 1) & 255
    kept = jnp.zeros((8, PIECE), jnp.float32)
    for n in range(DW // VBLK):
        same = jnp.where(irreps[y * (DW // VBLK) + n] == label, 1.0, 0.0)
        kept = jnp.where(lane >> 4 == n, same, kept)
    v_own[...] = (v_ref[...].astype(jnp.float32) * kept[0:1]).astype(jnp.bfloat16)

    m = lax.broadcasted_iota(jnp.int32, (1024, 128), 0)
    n = lax.broadcasted_iota(jnp.int32, (1024, 128), 1)
    hit = jnp.logical_and(m >> 7 == n >> 4, (m & 127) == (n & 15) + v * 16)
    pull[...] = jnp.where(hit, 1.0, 0.0).astype(jnp.bfloat16)
    for load in t_loads:
        load.wait()
    for c in range(CW):
        wide = jnp.concatenate([t_all[q, :, c * NV : c * NV + 128] for q in range(8)], axis=1)
        a_own[c] = dot(wide, pull[...]).astype(jnp.bfloat16)
    pl.semaphore_wait(barrier, 3 + 7 + 15 + 32 - first)

    names = {}
    sends = []

    def sem(*name):
        return names.setdefault(name, len(names))

    def hop(src, dst, where, *name):
        n = sem(*name)
        return remote(src, dst, ssem.at[n], rsem.at[n], where)

    def go(copy):
        copy.start()
        sends.append(copy)

    t_block = (3, 1)

    def t_rows(block, h):
        return t_all.at[pl.ds(block * 8 + k * 4 + h * 2, 2)]

    def t_copy(d, h):
        return hop(t_rows(0, h), t_rows(t_block[d], h), dev(x, y, zn[d], k), "t", d, h)

    def t_forward(d):
        return hop(t_rows(t_block[d], d), t_rows(2, d), dev(x, y, zn[d], k), "tf", d)

    def t_sibling(block, h):
        return hop(t_rows(block, h), t_rows(block, h), dev(x, y, z, 1 - k), "ts", block, h)

    def slab_place(block):
        rows = pl.ds(pl.multiple_of(y * 16, 16), 16)
        return a_mat.at[:, rows, pl.ds(pl.multiple_of(block * 128, 128), 128)]

    slab_rows = a_mat.at[:, pl.ds(pl.multiple_of(y * 16, 16), 16), :]

    def slab_y(d, s):
        slot = lax.rem(y + (NY - s if d == 0 else s), NY)
        part = a_mat.at[:, pl.ds(pl.multiple_of(slot * 16, 16), 16), :]
        return hop(part, part, dev(x, ys[d], z, k), "b", d, s)

    def v0_y(d, s):
        slot = s0.at[lax.rem(y + (NY - s if d == 0 else s), NY)]
        return hop(slot, slot, dev(x, ys[d], z, k), "v0y", d, s)

    def v0_rows(slot, part):
        return v_all.at[pl.ds(pl.multiple_of(slot * 64 + part * 16, 16), 16)]

    def v0_x(d, part):
        rows = v0_rows(x, part)
        return hop(rows, rows, dev(xs[d], y, z, k), "v0x", d, part)

    def v0_f(d):
        rows = v0_rows(xs[1 - d], d)
        return hop(rows, rows, dev(xs[d], y, z, k), "v0f", d)

    def v1_x(n):
        slot = s1.at[y, x]
        return hop(slot, slot, dev(lax.rem(x + n, NX), y, z, k), "v1x", n)

    def v1_y(d, s, e):
        slot = s1.at[lax.rem(y + (NY - s if d == 0 else s), NY), pl.ds(2 * e, 2)]
        return hop(slot, slot, dev(x, ys[d], z, k), "v1y", d, s, e)

    there = pick(v * 4 + zl, PLACE_OF)
    moves = there != z * 2 + k
    go_there = dev(x, y, lax.div(there, 2), lax.rem(there, 2))
    raw = [
        (v_own.at[pl.ds(0, 32)], s0.at[y], sem("r", 0)),
        (v_own.at[pl.ds(32, 32)], s1.at[y, x], sem("r", 1)),
    ]

    @pl.when(moves)
    def _():
        for src, dst, n in raw:
            remote(src, dst, ssem.at[n], rsem.at[n], go_there).start()

    @pl.when(jnp.logical_not(moves))
    def _():
        for src, dst, n in raw:
            pltpu.make_async_copy(src, dst, rsem.at[n]).start()

    for b in range(4):
        at = pick(v * 4 + b, PLACE_OF)
        az, ak = lax.div(at, 2), lax.rem(at, 2)
        block = lax.rem(zl - lax.rem(az, NZL) + NZL, NZL)
        mine = at == z * 2 + k

        @pl.when(mine)
        def _():
            pltpu.make_async_copy(a_own, slab_place(0), a_recv).start()

        @pl.when(jnp.logical_not(mine))
        def _():
            remote(a_own, slab_place(block), a_send, a_recv, dev(x, y, az, ak)).start()

    go(t_copy(0, 0))
    go(t_copy(1, 1))
    go(t_copy(0, 1))
    go(t_copy(1, 0))
    for src, dst, n in raw:
        pltpu.make_async_copy(src, dst, rsem.at[n]).wait()
        if n == raw[0][2]:
            go(v0_y(0, 0))
            go(v0_y(1, 0))
    for n in range(1, NX):
        go(v1_x(n))

    def v0_step(s):
        v0_y(0, s).wait_recv()
        if s < 3:
            go(v0_y(0, s + 1))
            v0_y(1, s).wait_recv()
        if s < 2:
            go(v0_y(1, s + 1))

    def v1_step(s):
        for e in range(2):
            for d in range(2):
                if s == 3 and d != e:
                    continue
                v1_y(d, s, e).wait_recv()
                if s < 2 or (s == 2 and d == e):
                    go(v1_y(d, s + 1, e))

    def slab_step(s):
        for d in range(2):
            if s == 3 and d == 1:
                continue
            slab_y(d, s).wait_recv()
            if s < 3 - d:
                go(slab_y(d, s + 1))

    def join(source, rows):
        for c in range(CW):
            for half in range(2):
                joined = jnp.concatenate(
                    [source[half * 4 + q][:, c * 256 : c * 256 + DW] for q in range(4)], axis=1
                )
                v_all[rows, c * NV + half * 896 : c * NV + (half + 1) * 896] = joined

    v0_step(0)
    for n in range(1, NX):
        v1_x(n).wait_recv()
    for e in range(2):
        go(v1_y(0, 0, e))
        go(v1_y(1, 0, e))
    v0_step(1)
    pltpu.make_async_copy(slab_rows, slab_rows, a_recv).wait()
    go(slab_y(0, 0))
    go(slab_y(1, 0))
    v0_step(2)
    t_copy(0, 0).wait_recv()
    go(t_forward(0))
    go(t_sibling(3, 0))
    t_copy(1, 1).wait_recv()
    go(t_forward(1))
    go(t_sibling(1, 1))
    v1_step(0)
    slab_step(0)
    v0_step(3)
    join([s0.at[q] for q in range(NY)], pl.ds(pl.multiple_of(x * 64, 32), 32))
    go(v0_x(0, 0))
    go(v0_x(1, 1))
    go(v0_x(0, 1))
    go(v0_x(1, 0))
    slab_step(1)
    m = lax.broadcasted_iota(jnp.int32, (256, 256), 0)
    n = lax.broadcasted_iota(jnp.int32, (256, 256), 1)
    hit = jnp.logical_and(m >> 4 == (n & 15), (m & 15) == n >> 4)
    swap[...] = jnp.where(hit, 1.0, 0.0).astype(jnp.bfloat16)
    lane = lax.broadcasted_iota(jnp.int32, (16, 256), 1)
    line = lax.broadcasted_iota(jnp.int32, (16, 256), 0)
    e_j = jnp.zeros((16, 256), jnp.float32)
    e_a = jnp.zeros((16, 256), jnp.float32)
    e_b = jnp.zeros((16, 256), jnp.float32)
    for n in range(16):
        e_j = jnp.where(line == n, occ[y * 16 + n], e_j)
        e_a = jnp.where(lane >> 4 == n, vir[blk_a * 16 + n], e_a)
        e_b = jnp.where((lane & 15) == n, vir[blk_b * 16 + n], e_b)
    for block in range(4):
        for q in range(8):
            e_i = occ[q * 16 + lax.rem(zl + block, NZL) * 4 + x]
            denom[block * 128 + q * 16 : block * 128 + q * 16 + 16, :] = ((e_i + e_j) - e_a) - e_b
    v1_step(1)
    slab_step(2)
    t_copy(0, 1).wait_recv()
    go(t_sibling(3, 1))
    t_copy(1, 0).wait_recv()
    go(t_sibling(1, 0))
    m = lax.broadcasted_iota(jnp.int32, (512, 512), 0)
    n = lax.broadcasted_iota(jnp.int32, (512, 512), 1)
    hit = jnp.logical_and((m >> 4 & 7) == n >> 6, m >> 7 == (n >> 4 & 3))
    hit = jnp.logical_and(hit, (m & 15) == (n & 15))
    order[...] = jnp.where(hit, 1.0, 0.0).astype(jnp.bfloat16)

    v0_x(0, 0).wait_recv()
    go(v0_f(0))
    v0_x(1, 1).wait_recv()
    go(v0_f(1))
    slab_step(3)
    v1_step(2)
    w_load.wait()
    zmat = None
    for c in range(CW):
        rows = w_own[:, c, pl.ds(pl.multiple_of(blk_b * 16, 16), 16), :].reshape(256, NO)
        part = dot(rows, a_mat[c])
        zmat = part if zmat is None else zmat + part
    for block in range(4):
        zs[block] = zmat[:, block * 128 : block * 128 + 128]
    chunk = lax.broadcasted_iota(jnp.int32, (16, 128), 1) >> 4

    def crossed(block, carry):
        for h in range(2):
            outs = [jnp.zeros((16, 128), jnp.float32)] * 8
            for b in range(8):
                part = zs[block, pl.ds(h * 8 + b, 16, stride=16), :]
                for q in range(8):
                    moved = pltpu.roll(part, (b - q) % 8 * 16, 1) if b != q else part
                    outs[q] = jnp.where(chunk == b, -moved, outs[q])
            for q in range(8):
                acc[h, pl.ds(pl.multiple_of(block * 128 + q * 16, 16), 16), :] = outs[q]
        return carry

    lax.fori_loop(0, 4, crossed, 0)

    v0_x(0, 1).wait_recv()
    v0_x(1, 0).wait_recv()
    for d in range(2):
        v0_f(d).wait_recv()
    v1_step(3)
    for slot in range(NX):
        join([s1.at[q, slot] for q in range(NY)], pl.ds(slot * 64 + 32, 32))
    for d in range(2):
        t_forward(d).wait_recv()
        go(t_sibling(2, d))
    for block in (3, 1):
        for h in range(2):
            t_sibling(block, h).wait_recv()

    def ladder(blocks, i):
        ks = pl.ds(pl.multiple_of(i * 768, 768), 768)
        for first_block, n in blocks:
            rows = pl.ds(first_block * 128, n * 128)
            both = dot(t_all[pl.ds(first_block * 8, n * 8), :, ks].reshape(n * 128, 768), v_all[:, ks], NT)
            for h in range(2):
                acc[h, rows, :] += both[:, h * 128 : h * 128 + 128]

    def ladder_most(i, carry):
        ladder(((0, 2), (3, 1)), i)
        return carry

    def ladder_last(i, carry):
        ladder(((2, 1),), i)
        return carry

    lax.fori_loop(0, KK // 768, ladder_most, 0)
    for h in range(2):
        t_sibling(2, h).wait_recv()
    lax.fori_loop(0, KK // 768, ladder_last, 0)

    def near(n):
        return lax.rem(zl + n, NZL)

    for half in range(2):
        for sj in (2 * half, 2 * half + 1):
            for si in range(4):
                for xj in range(4):
                    for h in range(2):
                        mail[pl.ds(xj * 256 + (sj * 4 + si) * 2 + h, 8, stride=32), :] = acc[
                            h, pl.ds(si * 128 + near(sj) * 4 + xj, 8, stride=16), :
                        ]

        def send_mail(n, carry):
            px, py = partner(n)
            src = mail.at[pl.ds(pl.multiple_of((px * 8 + py) * 32 + half * 16, 16), 16)]
            dst = rec.at[pl.ds(pl.multiple_of((x * 8 + y) * 32 + half * 16, 16), 16)]
            remote(src, dst, m_send.at[half], m_recv.at[half], dev(px, py, z, twin)).start()
            return carry

        lax.fori_loop(first, 32, send_mail, 0)

        @pl.when(diag)
        def _():
            here = pl.ds(pl.multiple_of((x * 8 + y) * 32 + half * 16, 16), 16)
            pltpu.make_async_copy(mail.at[here], rec.at[here], m_recv.at[half]).start()

    owner_z = lax.div(blk_a, 2) * NZL
    owner_k = lax.rem(blk_a, 2)

    for block in range(4):
        rows = pl.ds(block * 128, 128)
        turned = None
        for h in range(2):
            part = acc[h, rows, :]
            hi = part.astype(jnp.bfloat16)
            rest = part - hi.astype(jnp.float32)
            mid = rest.astype(jnp.bfloat16)
            low = (rest - mid.astype(jnp.float32)).astype(jnp.bfloat16)
            matrix = swap[h * 128 : h * 128 + 128, :]
            term = dot(hi, matrix) + (dot(mid, matrix) + dot(low, matrix))
            turned = term if turned is None else turned + term
        for h in range(2):
            own_x[h, rows, :] = turned[:, h * 128 : h * 128 + 128]

    for half in range(2):
        some = rec.at[pl.ds(0, 512)]
        pltpu.make_async_copy(some, some, m_recv.at[half]).wait()
        for sj in (2 * half, 2 * half + 1):
            for si in range(4):
                for xj in range(4):
                    for h in range(2):
                        rows = pl.ds(sj * 128 + near(si) * 4 + xj, 8, stride=16)
                        own_x[h, rows, :] += rec[pl.ds(xj * 256 + (sj * 4 + si) * 2 + h, 8, stride=32), :]
        for sj in (2 * half, 2 * half + 1):
            rows = pl.ds(sj * 128, 128)
            for h in range(2):
                lanes = pl.ds(h * 128, 128)
                sbuf[rows, lanes] = (own_x[h, rows, :] / denom[rows, lanes]).astype(jnp.bfloat16)
            target = owner_z + near(sj)
            n = sem("d", sj)
            if sj == 0:

                @pl.when(own)
                def _():
                    pltpu.make_async_copy(sbuf.at[rows], d_all.at[blk_b], d_recv).start()

                @pl.when(jnp.logical_not(own))
                def _():
                    remote(sbuf.at[rows], d_all.at[blk_b], ssem.at[n], d_recv, dev(x, y, target, owner_k)).start()
            else:
                go(remote(sbuf.at[rows], d_all.at[blk_b], ssem.at[n], d_recv, dev(x, y, target, owner_k)))

    pltpu.make_async_copy(d_all, d_all, d_recv).wait()
    for h in range(2):
        some = jnp.concatenate([d_all[b, :, h * 128 : h * 128 + 128] for b in range(4)], axis=1)
        out_ref[:, h * 512 : h * 512 + 512] = dot(some, order[...]).astype(jnp.bfloat16)

    for copy in sends:
        copy.wait_send()

    @pl.when(moves)
    def _():
        for src, dst, n in raw:
            pltpu.make_async_copy(src, src, ssem.at[n]).wait()

    @pl.when(jnp.logical_not(own))
    def _():
        some = sbuf.at[pl.ds(0, 128)]
        pltpu.make_async_copy(some, some, ssem.at[sem("d", 0)]).wait()

    three = a_mat.at[:, pl.ds(0, 16), pl.ds(0, 384)]

    @pl.when(own)
    def _():
        pltpu.make_async_copy(three, three, a_send).wait()

    @pl.when(jnp.logical_not(own))
    def _():
        pltpu.make_async_copy(slab_rows, slab_rows, a_send).wait()

    @pl.when(diag)
    def _():
        for half in range(2):
            some = rec.at[pl.ds(0, 31 * 16)]
            pltpu.make_async_copy(some, some, m_send.at[half]).wait()

    @pl.when(jnp.logical_not(diag))
    def _():
        for half in range(2):
            some = rec.at[pl.ds(0, 512)]
            pltpu.make_async_copy(some, some, m_send.at[half]).wait()


def call(t, vv, w, irreps, occ, vir):
    bf, f32 = jnp.bfloat16, jnp.float32
    vm = pl.BlockSpec(memory_space=pltpu.VMEM)
    smem = pl.BlockSpec(memory_space=pltpu.SMEM)
    anywhere = pl.BlockSpec(memory_space=pl.ANY)
    dma = pltpu.SemaphoreType.DMA
    return pl.pallas_call(
        kernel,
        out_shape=jax.ShapeDtypeStruct((NO, 1024), bf),
        in_specs=[anywhere, vm, anywhere, smem, smem, smem],
        out_specs=vm,
        scratch_shapes=[
            pltpu.VMEM((32, 16, KK), bf),
            pltpu.VMEM((NY, 32, PIECE), bf),
            pltpu.VMEM((NY, NX, 32, PIECE), bf),
            pltpu.VMEM((256, KK), bf),
            pltpu.VMEM((CW, NO, 512), bf),
            pltpu.VMEM((4, 256, 128), f32),
            pltpu.VMEM((2, 512, 128), f32),
            pltpu.VMEM((2, 512, 128), f32),
            pltpu.VMEM((512, 512), bf),
            pltpu.VMEM((256, 256), bf),
            pltpu.VMEM((1024, 128), bf),
            pltpu.VMEM((CW, 16, 128), bf),
            pltpu.VMEM((64, PIECE), bf),
            pltpu.VMEM((16, CW, SA, NO), bf),
            pltpu.VMEM((512, 256), f32),
            pltpu.VMEM((1024, 128), f32),
            pltpu.VMEM((1024, 128), f32),
            pltpu.VMEM((512, 256), bf),
            pltpu.VMEM((4, 128, 256), bf),
            dma((80,)), dma((80,)), dma((4,)), dma, dma, dma((2,)), dma((2,)), dma,
        ],
        compiler_params=pltpu.CompilerParams(
            collective_id=0, has_side_effects=True, vmem_limit_bytes=64 * 1024 * 1024
        ),
        cost_estimate=pl.CostEstimate(flops=2 * 512 * 256 * KK, bytes_accessed=20_000_000, transcendentals=0),
    )(t, vv, w, irreps, occ, vir)


def local(amplitudes, integrals, hole_integrals, irreps, occ_energy, vir_energy):
    t = jnp.transpose(amplitudes.reshape(8, 16, CW, NV), (0, 2, 1, 3))
    vv = jnp.transpose(integrals, (1, 0, 2, 3)).reshape(64, CW, DW)
    vv = jnp.pad(vv, ((0, 0), (0, 0), (0, 256 - DW))).reshape(64, PIECE)
    w = jnp.transpose(hole_integrals.reshape(NO, 16, CW, SA), (1, 2, 3, 0))
    out = call(t, vv, w, irreps, occ_energy, vir_energy)
    return out.reshape(8, 1, 1, 1, 16, 16, SA)


def solution(mesh):
    in_specs = (
        P(None, "row", None, "col", None, None, None),
        P("vir", "row", None, "col"),
        P(None, None, "col", None, None, None),
        P(),
        P(),
        P(),
    )
    out_specs = P(None, "row", None, "col", None, "vir", None)
    return jax.shard_map(local, mesh=mesh, in_specs=in_specs, out_specs=out_specs, check_vma=False)
```

```python
import jax
import jax.numpy as jnp
from jax import lax
from jax.experimental import pallas as pl
from jax.experimental.pallas import tpu as pltpu
from jax.sharding import PartitionSpec as P

NO = 128
NV = 1792
SA = 64
CW = 3
VBLK = 16
KK = CW * NV
NX, NY, NZ, NZL = 4, 8, 8, 4
DW = NV // NY
PIECE = CW * 256
MESH = pl.DeviceIdType.MESH
NT = (((1,), (1,)), ((), ()))
NN = (((1,), (0,)), ((), ()))

WORK = [
    (0, 1), (1, 0), (0, 0), (1, 1), (2, 1), (1, 2), (0, 3), (3, 0),
    (2, 0), (0, 2), (1, 3), (3, 1), (2, 2), (3, 3), (2, 3), (3, 2),
]
ABOVE = (0, 3, 1, 2)
PLACE_OF = [WORK.index((a, b)) for a in range(4) for b in range(4)]


def pick(index, table):
    value = jnp.int32(table[0])
    for n in range(1, len(table)):
        value = jnp.where(index == n, jnp.int32(table[n]), value)
    return value


def dev(x, y, z, k):
    return (lax.rem(z, NZL) * NX + x, y, lax.div(z, NZL) * 2 + k)


def dot(a, b, dims=NN):
    return lax.dot_general(a, b, dims, preferred_element_type=jnp.float32)


def remote(src, dst, send, recv, where):
    return pltpu.make_async_remote_copy(
        src_ref=src, dst_ref=dst, send_sem=send, recv_sem=recv, device_id=where, device_id_type=MESH
    )


def kernel(
    t_ref, v_ref, w_ref, irreps, occ, vir, out_ref,
    t_all, s0, s1, v_all, a_mat, zs, acc, own_x, order, swap, pull, a_own, v_own, w_own, denom, mail, rec, sbuf, d_all,
    ssem, rsem, load_sem, a_send, a_recv, m_send, m_recv, d_recv,
):
    r = lax.axis_index("row")
    y = lax.axis_index("col")
    v = lax.axis_index("vir")
    x, zl = lax.rem(r, NX), lax.div(r, NX)
    zh, k = lax.div(v, 2), lax.rem(v, 2)
    z = zh * NZL + zl
    xs = (lax.rem(x + 1, NX), lax.rem(x + NX - 1, NX))
    ys = (lax.rem(y + 1, NY), lax.rem(y + NY - 1, NY))
    zn = (lax.rem(z + 1, NZ), lax.rem(z + NZ - 1, NZ))
    blk_a = pick(z * 2 + k, [w[0] for w in WORK])
    blk_b = pick(z * 2 + k, [w[1] for w in WORK])
    diag = blk_a == blk_b
    own = blk_a == v
    twin = jnp.where(diag, k, 1 - k)

    t_loads = [
        pltpu.make_async_copy(
            t_ref.at[:, c], t_all.at[pl.ds(0, 8), :, pl.ds(c * NV, NV)], load_sem.at[c]
        )
        for c in range(CW)
    ]
    w_load = pltpu.make_async_copy(w_ref, w_own, load_sem.at[3])
    for load in t_loads:
        load.start()
    w_load.start()

    barrier = pltpu.get_barrier_semaphore()

    def greet(where):
        pl.semaphore_signal(barrier, inc=1, device_id=where, device_id_type=MESH)

    for n in range(1, NX):
        greet(dev(lax.rem(x + n, NX), y, z, k))

    def greet_y(n, carry):
        greet(dev(x, lax.rem(y + n, NY), z, k))
        return carry

    lax.fori_loop(1, NY, greet_y, 0)

    def greet_z(n, carry):
        other = lax.rem(z * 2 + k + n, 16)
        greet(dev(x, y, lax.div(other, 2), lax.rem(other, 2)))
        return carry

    lax.fori_loop(1, 16, greet_z, 0)
    first = jnp.where(diag, 1, 0)

    def partner(n):
        m = lax.div(n, NX)
        far = jnp.where(lax.rem(m, 2) == 1, 4 - lax.div(m + 1, 2), 4 + lax.div(m, 2))
        return (lax.rem(x + 3 - lax.rem(n, NX), NX), lax.rem(y + far, NY))

    def greet_mail(n, carry):
        px, py = partner(n)
        greet(dev(px, py, z, twin))
        return carry

    lax.fori_loop(0, 32 - first, greet_mail, 0)
    label = jnp.bitwise_xor(jnp.bitwise_xor(irreps[v], irreps[zl]), irreps[0])
    lane = lax.broadcasted_iota(jnp.int32, (8, PIECE), 1) & 255
    kept = jnp.zeros((8, PIECE), jnp.float32)
    for n in range(DW // VBLK):
        same = jnp.where(irreps[y * (DW // VBLK) + n] == label, 1.0, 0.0)
        kept = jnp.where(lane >> 4 == n, same, kept)
    v_own[...] = (v_ref[...].astype(jnp.float32) * kept[0:1]).astype(jnp.bfloat16)

    m = lax.broadcasted_iota(jnp.int32, (1024, 128), 0)
    n = lax.broadcasted_iota(jnp.int32, (1024, 128), 1)
    hit = jnp.logical_and(m >> 7 == n >> 4, (m & 127) == (n & 15) + v * 16)
    pull[...] = jnp.where(hit, 1.0, 0.0).astype(jnp.bfloat16)
    for load in t_loads:
        load.wait()
    wide = jnp.concatenate(
        [
            jnp.concatenate([t_all[q, :, c * NV : c * NV + 128] for q in range(8)], axis=1)
            for c in range(CW)
        ],
        axis=0,
    )
    a_own[...] = dot(wide, pull[...]).astype(jnp.bfloat16).reshape(CW, 16, 128)
    pl.semaphore_wait(barrier, 3 + 7 + 15 + 32 - first)

    names = {}
    sends = []

    def sem(*name):
        return names.setdefault(name, len(names))

    def hop(src, dst, where, *name):
        n = sem(*name)
        return remote(src, dst, ssem.at[n], rsem.at[n], where)

    def go(copy):
        copy.start()
        sends.append(copy)

    t_block = (1, 2)

    def t_rows(block, u):
        return t_all.at[pl.ds(block * 8 + k * 4 + u, 1)]

    def t_copy(d, i):
        u = 3 * d + (1 - 2 * d) * i
        return hop(t_rows(0, u), t_rows(t_block[d], u), dev(x, y, zn[d], k), "t", d, i)

    def t_forward(d, i):
        u = 3 * d + (1 - 2 * d) * i
        return hop(t_rows(t_block[d], u), t_rows(3, u), dev(x, y, zn[d], k), "tf", d, i)

    def t_sibling(block, u):
        return hop(t_rows(block, u), t_rows(block, u), dev(x, y, z, 1 - k), "ts", block, u)

    def t_start(i):
        for d in range(2):
            go(t_copy(d, i))

    def t_step(i):
        for d in range(2):
            t_copy(d, i).wait_recv()
            if i < 2:
                go(t_forward(d, i))
            go(t_sibling(t_block[d], 3 * d + (1 - 2 * d) * i))

    def t_last(i):
        for d in range(2):
            t_forward(d, i).wait_recv()
            go(t_sibling(3, 3 * d + (1 - 2 * d) * i))

    def slab_place(block):
        rows = pl.ds(pl.multiple_of(y * 16, 16), 16)
        return a_mat.at[:, rows, pl.ds(pl.multiple_of(block * 128, 128), 128)]

    slab_rows = a_mat.at[:, pl.ds(pl.multiple_of(y * 16, 16), 16), :]

    def slab_y(d, s):
        slot = lax.rem(y + (NY - s if d == 0 else s), NY)
        part = a_mat.at[:, pl.ds(pl.multiple_of(slot * 16, 16), 16), :]
        return hop(part, part, dev(x, ys[d], z, k), "b", d, s)

    def v0_y(d, s):
        slot = s0.at[lax.rem(y + (NY - s if d == 0 else s), NY)]
        return hop(slot, slot, dev(x, ys[d], z, k), "v0y", d, s)

    def v0_rows(slot, part):
        return v_all.at[pl.ds(pl.multiple_of(slot * 64 + part * 16, 16), 16)]

    def v0_x(d, part):
        rows = v0_rows(x, part)
        return hop(rows, rows, dev(xs[d], y, z, k), "v0x", d, part)

    def v0_f(d):
        rows = v0_rows(xs[1 - d], d)
        return hop(rows, rows, dev(xs[d], y, z, k), "v0f", d)

    def v1_x(n):
        slot = s1.at[y, x]
        return hop(slot, slot, dev(lax.rem(x + n, NX), y, z, k), "v1x", n)

    def v1_y(d, s, e):
        slot = s1.at[lax.rem(y + (NY - s if d == 0 else s), NY), pl.ds(2 * e, 2)]
        return hop(slot, slot, dev(x, ys[d], z, k), "v1y", d, s, e)

    there = pick(v * 4 + zl, PLACE_OF)
    moves = there != z * 2 + k
    go_there = dev(x, y, lax.div(there, 2), lax.rem(there, 2))
    raw = [
        (v_own.at[pl.ds(0, 32)], s0.at[y], sem("r", 0)),
        (v_own.at[pl.ds(32, 32)], s1.at[y, x], sem("r", 1)),
    ]

    @pl.when(moves)
    def _():
        for src, dst, n in raw:
            remote(src, dst, ssem.at[n], rsem.at[n], go_there).start()

    @pl.when(jnp.logical_not(moves))
    def _():
        for src, dst, n in raw:
            pltpu.make_async_copy(src, dst, rsem.at[n]).start()

    for b in range(4):
        at = pick(v * 4 + b, PLACE_OF)
        az, ak = lax.div(at, 2), lax.rem(at, 2)
        above = lax.rem(zl - lax.rem(az, NZL) + NZL, NZL)
        block = jnp.where(above == 0, 0, jnp.where(above == 3, 1, above + 1))
        mine = at == z * 2 + k

        @pl.when(mine)
        def _():
            pltpu.make_async_copy(a_own, slab_place(0), a_recv).start()

        @pl.when(jnp.logical_not(mine))
        def _():
            remote(a_own, slab_place(block), a_send, a_recv, dev(x, y, az, ak)).start()

    t_start(0)
    t_start(1)
    for src, dst, n in raw:
        pltpu.make_async_copy(src, dst, rsem.at[n]).wait()
        if n == raw[0][2]:
            go(v0_y(0, 0))
            go(v0_y(1, 0))
    for n in range(1, NX):
        go(v1_x(n))

    def v0_step(s):
        v0_y(0, s).wait_recv()
        if s < 3:
            go(v0_y(0, s + 1))
            v0_y(1, s).wait_recv()
        if s < 2:
            go(v0_y(1, s + 1))

    def v1_step(s):
        for e in range(2):
            for d in range(2):
                if s == 3 and d != e:
                    continue
                v1_y(d, s, e).wait_recv()
                if s < 2 or (s == 2 and d == e):
                    go(v1_y(d, s + 1, e))

    def slab_step(s):
        for d in range(2):
            if s == 3 and d == 1:
                continue
            slab_y(d, s).wait_recv()
            if s < 3 - d:
                go(slab_y(d, s + 1))

    def join(source, rows, half):
        for c in range(CW):
            joined = jnp.concatenate([source(half * 4 + q, c) for q in range(4)], axis=1)
            v_all[rows, pl.ds(pl.multiple_of(c * NV + half * 896, 128), 896)] = joined

    def join0(half):
        rows = pl.ds(pl.multiple_of(x * 64, 32), 32)
        join(lambda q, c: s0[q, :, c * 256 : c * 256 + DW], rows, half)

    def join1(half):
        for slot in range(NX):
            join(lambda q, c: s1[q, slot, :, c * 256 : c * 256 + DW], pl.ds(slot * 64 + 32, 32), half)

    near_half = lax.div(y, 4)
    v0_step(0)
    for n in range(1, NX):
        v1_x(n).wait_recv()
    for e in range(2):
        go(v1_y(0, 0, e))
        go(v1_y(1, 0, e))
    v0_step(1)
    pltpu.make_async_copy(slab_rows, slab_rows, a_recv).wait()
    go(slab_y(0, 0))
    go(slab_y(1, 0))
    v0_step(2)
    t_step(0)
    t_start(2)
    v1_step(0)
    t_step(1)
    t_start(3)
    v0_step(3)
    for half in range(2):
        join0(half)
    go(v0_x(0, 0))
    go(v0_x(1, 1))
    go(v0_x(0, 1))
    go(v0_x(1, 0))
    slab_step(0)
    m = lax.broadcasted_iota(jnp.int32, (256, 256), 0)
    n = lax.broadcasted_iota(jnp.int32, (256, 256), 1)
    hit = jnp.logical_and(m >> 4 == (n & 15), (m & 15) == n >> 4)
    swap[...] = jnp.where(hit, 1.0, 0.0).astype(jnp.bfloat16)
    lane = lax.broadcasted_iota(jnp.int32, (16, 256), 1)
    line = lax.broadcasted_iota(jnp.int32, (16, 256), 0)
    e_j = jnp.zeros((16, 256), jnp.float32)
    e_a = jnp.zeros((16, 256), jnp.float32)
    e_b = jnp.zeros((16, 256), jnp.float32)
    for n in range(16):
        e_j = jnp.where(line == n, occ[y * 16 + n], e_j)
        e_a = jnp.where(lane >> 4 == n, vir[blk_a * 16 + n], e_a)
        e_b = jnp.where((lane & 15) == n, vir[blk_b * 16 + n], e_b)
    for block in range(4):
        for q in range(8):
            e_i = occ[q * 16 + lax.rem(zl + ABOVE[block], NZL) * 4 + x]
            denom[block * 128 + q * 16 : block * 128 + q * 16 + 16, :] = ((e_i + e_j) - e_a) - e_b
    v1_step(1)
    slab_step(1)
    m = lax.broadcasted_iota(jnp.int32, (512, 512), 0)
    n = lax.broadcasted_iota(jnp.int32, (512, 512), 1)
    hit = jnp.logical_and((m >> 4 & 7) == n >> 6, m >> 7 == (n >> 4 & 3))
    hit = jnp.logical_and(hit, (m & 15) == (n & 15))
    order[...] = jnp.where(hit, 1.0, 0.0).astype(jnp.bfloat16)

    v0_x(0, 0).wait_recv()
    go(v0_f(0))
    v0_x(1, 1).wait_recv()
    go(v0_f(1))
    slab_step(2)
    t_step(2)
    v1_step(2)
    slab_step(3)
    w_load.wait()
    zmat = None
    for c in range(CW):
        rows = w_own[:, c, pl.ds(pl.multiple_of(blk_b * 16, 16), 16), :].reshape(256, NO)
        part = dot(rows, a_mat[c])
        zmat = part if zmat is None else zmat + part
    for block in range(4):
        zs[block] = zmat[:, block * 128 : block * 128 + 128]
    chunk = lax.broadcasted_iota(jnp.int32, (16, 128), 1) >> 4

    def crossed(block, carry):
        for h in range(2):
            outs = [jnp.zeros((16, 128), jnp.float32)] * 8
            for b in range(8):
                part = zs[block, pl.ds(h * 8 + b, 16, stride=16), :]
                for q in range(8):
                    moved = pltpu.roll(part, (b - q) % 8 * 16, 1) if b != q else part
                    outs[q] = jnp.where(chunk == b, -moved, outs[q])
            for q in range(8):
                acc[h, pl.ds(pl.multiple_of(block * 128 + q * 16, 16), 16), :] = outs[q]
        return carry

    lax.fori_loop(0, 4, crossed, 0)

    t_step(3)
    t_last(0)
    v0_x(0, 1).wait_recv()
    v0_x(1, 0).wait_recv()
    for d in range(2):
        v0_f(d).wait_recv()
    join1(near_half)
    v1_step(3)
    t_last(1)
    join1(1 - near_half)
    for u in range(4):
        t_sibling(1, u).wait_recv()

    def ladder(pair):
        def step(i, carry):
            ks = pl.ds(pl.multiple_of(i * 1792, 1792), 1792)
            both = dot(t_all[pl.ds(pair * 16, 16), :, ks].reshape(256, 1792), v_all[:, ks], NT)
            for h in range(2):
                acc[h, pl.ds(pair * 256, 256), :] += both[:, h * 128 : h * 128 + 128]
            return carry

        lax.fori_loop(0, KK // 1792, step, 0)

    def near(n):
        return lax.rem(zl + ABOVE[n], NZL)

    def tile_row(si, sj, h):
        return (si // 2 * 2 + sj // 2) * 8 + (si % 2 * 2 + sj % 2) * 2 + h

    def fill(pair, half):
        for si in (2 * pair, 2 * pair + 1):
            for sj in (2 * half, 2 * half + 1):
                for xj in range(4):
                    for h in range(2):
                        mail[pl.ds(xj * 256 + tile_row(si, sj, h), 8, stride=32), :] = acc[
                            h, pl.ds(si * 128 + near(sj) * 4 + xj, 8, stride=16), :
                        ]

    def post(part, start, rows):
        def send_mail(n, carry):
            px, py = partner(n)
            src = mail.at[pl.ds(pl.multiple_of((px * 8 + py) * 32 + start, 8), rows)]
            dst = rec.at[pl.ds(pl.multiple_of((x * 8 + y) * 32 + start, 8), rows)]
            remote(src, dst, m_send.at[part], m_recv.at[part], dev(px, py, z, twin)).start()
            return carry

        lax.fori_loop(0, 32 - first, send_mail, 0)

        @pl.when(diag)
        def _():
            here = pl.ds(pl.multiple_of((x * 8 + y) * 32 + start, 8), rows)
            pltpu.make_async_copy(mail.at[here], rec.at[here], m_recv.at[part]).start()

    ladder(0)
    fill(0, 0)
    fill(0, 1)
    post(0, 0, 16)
    for block in (2, 3):
        for u in range(4):
            t_sibling(block, u).wait_recv()
    ladder(1)
    fill(1, 0)
    post(1, 16, 8)
    fill(1, 1)
    post(2, 24, 8)

    owner_z = lax.div(blk_a, 2) * NZL
    owner_k = lax.rem(blk_a, 2)
    for block in range(4):
        rows = pl.ds(block * 128, 128)
        turned = None
        for h in range(2):
            part = acc[h, rows, :]
            hi = part.astype(jnp.bfloat16)
            rest = part - hi.astype(jnp.float32)
            mid = rest.astype(jnp.bfloat16)
            low = (rest - mid.astype(jnp.float32)).astype(jnp.bfloat16)
            matrix = swap[h * 128 : h * 128 + 128, :]
            term = dot(hi, matrix) + (dot(mid, matrix) + dot(low, matrix))
            turned = term if turned is None else turned + term
        for h in range(2):
            own_x[h, rows, :] = turned[:, h * 128 : h * 128 + 128]

    def arrived(part, count):
        some = rec.at[pl.ds(0, count)]
        pltpu.make_async_copy(some, some, m_recv.at[part]).wait()

    def take(pair, half):
        for si in (2 * pair, 2 * pair + 1):
            for sj in (2 * half, 2 * half + 1):
                for xj in range(4):
                    for h in range(2):
                        rows = pl.ds(sj * 128 + near(si) * 4 + xj, 8, stride=16)
                        own_x[h, rows, :] += rec[pl.ds(xj * 256 + tile_row(si, sj, h), 8, stride=32), :]

    arrived(0, 512)
    take(0, 0)
    take(0, 1)
    for half in range(2):
        arrived(1 + half, 256)
        take(1, half)
        for sj in (2 * half, 2 * half + 1):
            rows = pl.ds(sj * 128, 128)
            for h in range(2):
                lanes = pl.ds(h * 128, 128)
                sbuf[rows, lanes] = (own_x[h, rows, :] / denom[rows, lanes]).astype(jnp.bfloat16)
            target = owner_z + near(sj)
            n = sem("d", sj)
            if sj == 0:

                @pl.when(own)
                def _():
                    pltpu.make_async_copy(sbuf.at[rows], d_all.at[blk_b], d_recv).start()

                @pl.when(jnp.logical_not(own))
                def _():
                    remote(sbuf.at[rows], d_all.at[blk_b], ssem.at[n], d_recv, dev(x, y, target, owner_k)).start()
            else:
                go(remote(sbuf.at[rows], d_all.at[blk_b], ssem.at[n], d_recv, dev(x, y, target, owner_k)))

    pltpu.make_async_copy(d_all, d_all, d_recv).wait()
    for h in range(2):
        some = jnp.concatenate([d_all[b, :, h * 128 : h * 128 + 128] for b in range(4)], axis=1)
        out_ref[:, h * 512 : h * 512 + 512] = dot(some, order[...]).astype(jnp.bfloat16)

    for copy in sends:
        copy.wait_send()

    @pl.when(moves)
    def _():
        for src, dst, n in raw:
            pltpu.make_async_copy(src, src, ssem.at[n]).wait()

    @pl.when(jnp.logical_not(own))
    def _():
        some = sbuf.at[pl.ds(0, 128)]
        pltpu.make_async_copy(some, some, ssem.at[sem("d", 0)]).wait()

    three = a_mat.at[:, pl.ds(0, 16), pl.ds(0, 384)]

    @pl.when(own)
    def _():
        pltpu.make_async_copy(three, three, a_send).wait()

    @pl.when(jnp.logical_not(own))
    def _():
        pltpu.make_async_copy(slab_rows, slab_rows, a_send).wait()

    for part, rows in ((0, 16), (1, 8), (2, 8)):

        @pl.when(diag)
        def _():
            some = rec.at[pl.ds(0, 31 * rows)]
            pltpu.make_async_copy(some, some, m_send.at[part]).wait()

        @pl.when(jnp.logical_not(diag))
        def _():
            some = rec.at[pl.ds(0, 32 * rows)]
            pltpu.make_async_copy(some, some, m_send.at[part]).wait()


def call(t, vv, w, irreps, occ, vir):
    bf, f32 = jnp.bfloat16, jnp.float32
    vm = pl.BlockSpec(memory_space=pltpu.VMEM)
    smem = pl.BlockSpec(memory_space=pltpu.SMEM)
    anywhere = pl.BlockSpec(memory_space=pl.ANY)
    dma = pltpu.SemaphoreType.DMA
    return pl.pallas_call(
        kernel,
        out_shape=jax.ShapeDtypeStruct((NO, 1024), bf),
        in_specs=[anywhere, vm, anywhere, smem, smem, smem],
        out_specs=vm,
        scratch_shapes=[
            pltpu.VMEM((32, 16, KK), bf),
            pltpu.VMEM((NY, 32, PIECE), bf),
            pltpu.VMEM((NY, NX, 32, PIECE), bf),
            pltpu.VMEM((256, KK), bf),
            pltpu.VMEM((CW, NO, 512), bf),
            pltpu.VMEM((4, 256, 128), f32),
            pltpu.VMEM((2, 512, 128), f32),
            pltpu.VMEM((2, 512, 128), f32),
            pltpu.VMEM((512, 512), bf),
            pltpu.VMEM((256, 256), bf),
            pltpu.VMEM((1024, 128), bf),
            pltpu.VMEM((CW, 16, 128), bf),
            pltpu.VMEM((64, PIECE), bf),
            pltpu.VMEM((16, CW, SA, NO), bf),
            pltpu.VMEM((512, 256), f32),
            pltpu.VMEM((1024, 128), f32),
            pltpu.VMEM((1024, 128), f32),
            pltpu.VMEM((512, 256), bf),
            pltpu.VMEM((4, 128, 256), bf),
            dma((96,)), dma((96,)), dma((4,)), dma, dma, dma((3,)), dma((3,)), dma,
        ],
        compiler_params=pltpu.CompilerParams(
            collective_id=0, has_side_effects=True, vmem_limit_bytes=64 * 1024 * 1024
        ),
        cost_estimate=pl.CostEstimate(flops=2 * 512 * 256 * KK, bytes_accessed=20_000_000, transcendentals=0),
    )(t, vv, w, irreps, occ, vir)


def local(amplitudes, integrals, hole_integrals, irreps, occ_energy, vir_energy):
    t = jnp.transpose(amplitudes.reshape(8, 16, CW, NV), (0, 2, 1, 3))
    vv = jnp.transpose(integrals, (1, 0, 2, 3)).reshape(64, CW, DW)
    vv = jnp.pad(vv, ((0, 0), (0, 0), (0, 256 - DW))).reshape(64, PIECE)
    w = jnp.transpose(hole_integrals.reshape(NO, 16, CW, SA), (1, 2, 3, 0))
    out = call(t, vv, w, irreps, occ_energy, vir_energy)
    return out.reshape(8, 1, 1, 1, 16, 16, SA)


def solution(mesh):
    in_specs = (
        P(None, "row", None, "col", None, None, None),
        P("vir", "row", None, "col"),
        P(None, None, "col", None, None, None),
        P(),
        P(),
        P(),
    )
    out_specs = P(None, "row", None, "col", None, "vir", None)
    return jax.shard_map(local, mesh=mesh, in_specs=in_specs, out_specs=out_specs, check_vma=False)
```

```python
import jax
import jax.numpy as jnp
from jax import lax
from jax.experimental import pallas as pl
from jax.experimental.pallas import tpu as pltpu
from jax.sharding import PartitionSpec as P

NO = 128
NV = 1792
SA = 64
CW = 3
VBLK = 16
KK = CW * NV
NX, NY, NZ, NZL = 4, 8, 8, 4
DW = NV // NY
PIECE = CW * 256
MESH = pl.DeviceIdType.MESH
NT = (((1,), (1,)), ((), ()))
NN = (((1,), (0,)), ((), ()))

WORK = [
    (0, 1), (1, 0), (0, 0), (1, 1), (2, 1), (1, 2), (0, 3), (3, 0),
    (2, 0), (0, 2), (1, 3), (3, 1), (2, 2), (3, 3), (2, 3), (3, 2),
]
ABOVE = (0, 3, 1, 2)
PLACE_OF = [WORK.index((a, b)) for a in range(4) for b in range(4)]


def pick(index, table):
    value = jnp.int32(table[0])
    for n in range(1, len(table)):
        value = jnp.where(index == n, jnp.int32(table[n]), value)
    return value


def dev(x, y, z, k):
    return (lax.rem(z, NZL) * NX + x, y, lax.div(z, NZL) * 2 + k)


def dot(a, b, dims=NN):
    return lax.dot_general(a, b, dims, preferred_element_type=jnp.float32)


def remote(src, dst, send, recv, where):
    return pltpu.make_async_remote_copy(
        src_ref=src, dst_ref=dst, send_sem=send, recv_sem=recv, device_id=where, device_id_type=MESH
    )


def kernel(
    t_ref, v_ref, w_ref, irreps, occ, vir, out_ref,
    t_all, s0, x1, s1, v_all, a_mat, zs, acc, own_x, order, swap, pull, a_own, v_raw, v_own, w_own, denom, mail, rec, sbuf, d_all,
    ssem, rsem, load_sem, a_send, a_recv, m_send, m_recv, d_recv,
):
    r = lax.axis_index("row")
    y = lax.axis_index("col")
    v = lax.axis_index("vir")
    x, zl = lax.rem(r, NX), lax.div(r, NX)
    zh, k = lax.div(v, 2), lax.rem(v, 2)
    z = zh * NZL + zl
    xs = (lax.rem(x + 1, NX), lax.rem(x + NX - 1, NX))
    ys = (lax.rem(y + 1, NY), lax.rem(y + NY - 1, NY))
    zn = (lax.rem(z + 1, NZ), lax.rem(z + NZ - 1, NZ))
    blk_a = pick(z * 2 + k, [w[0] for w in WORK])
    blk_b = pick(z * 2 + k, [w[1] for w in WORK])
    diag = blk_a == blk_b
    own = blk_a == v
    twin = jnp.where(diag, k, 1 - k)

    t_loads = [
        pltpu.make_async_copy(
            t_ref.at[:, c], t_all.at[pl.ds(0, 8), :, pl.ds(c * NV, NV)], load_sem.at[c]
        )
        for c in range(CW)
    ]
    w_load = pltpu.make_async_copy(w_ref, w_own, load_sem.at[3])
    for load in t_loads:
        load.start()
    w_load.start()
    v_load = pltpu.make_async_copy(v_ref, v_raw, load_sem.at[4])
    v_load.start()

    barrier = pltpu.get_barrier_semaphore()

    def greet(where):
        pl.semaphore_signal(barrier, inc=1, device_id=where, device_id_type=MESH)

    for n in range(1, NX):
        greet(dev(lax.rem(x + n, NX), y, z, k))

    def greet_y(n, carry):
        greet(dev(x, lax.rem(y + n, NY), z, k))
        return carry

    lax.fori_loop(1, NY, greet_y, 0)

    def greet_z(n, carry):
        other = lax.rem(z * 2 + k + n, 16)
        greet(dev(x, y, lax.div(other, 2), lax.rem(other, 2)))
        return carry

    lax.fori_loop(1, 16, greet_z, 0)
    first = jnp.where(diag, 1, 0)

    def partner(n):
        m = lax.div(n, NX)
        far = jnp.where(lax.rem(m, 2) == 1, 4 - lax.div(m + 1, 2), 4 + lax.div(m, 2))
        return (lax.rem(x + 3 - lax.rem(n, NX), NX), lax.rem(y + far, NY))

    def greet_mail(n, carry):
        px, py = partner(n)
        greet(dev(px, py, z, twin))
        return carry

    lax.fori_loop(0, 32 - first, greet_mail, 0)
    label = jnp.bitwise_xor(jnp.bitwise_xor(irreps[v], irreps[zl]), irreps[0])
    lane = lax.broadcasted_iota(jnp.int32, (8, PIECE), 1) & 255
    kept = jnp.zeros((8, PIECE), jnp.float32)
    for n in range(DW // VBLK):
        same = jnp.where(irreps[y * (DW // VBLK) + n] == label, 1.0, 0.0)
        kept = jnp.where(lane >> 4 == n, same, kept)
    v_own[...] = jnp.zeros_like(v_own)
    v_load.wait()
    for b in range(4):
        for c in range(CW):
            part = v_raw[:, c, b, :].astype(jnp.float32) * kept[0:1, :DW]
            v_own[b * 16 : b * 16 + 16, c * 256 : c * 256 + DW] = part.astype(jnp.bfloat16)

    m = lax.broadcasted_iota(jnp.int32, (1024, 128), 0)
    n = lax.broadcasted_iota(jnp.int32, (1024, 128), 1)
    hit = jnp.logical_and(m >> 7 == n >> 4, (m & 127) == (n & 15) + v * 16)
    pull[...] = jnp.where(hit, 1.0, 0.0).astype(jnp.bfloat16)
    for load in t_loads:
        load.wait()
    wide = jnp.concatenate(
        [
            jnp.concatenate([t_all[q, :, c * NV : c * NV + 128] for q in range(8)], axis=1)
            for c in range(CW)
        ],
        axis=0,
    )
    a_own[...] = dot(wide, pull[...]).astype(jnp.bfloat16).reshape(CW, 16, 128)
    pl.semaphore_wait(barrier, 3 + 7 + 15 + 32 - first)

    names = {}
    sends = []

    def sem(*name):
        return names.setdefault(name, len(names))

    def hop(src, dst, where, *name):
        n = sem(*name)
        return remote(src, dst, ssem.at[n], rsem.at[n], where)

    def go(copy):
        copy.start()
        sends.append(copy)

    t_block = (1, 2)

    def t_rows(block, u):
        return t_all.at[pl.ds(block * 8 + k * 4 + u, 1)]

    def t_copy(d, i):
        u = 3 * d + (1 - 2 * d) * i
        return hop(t_rows(0, u), t_rows(t_block[d], u), dev(x, y, zn[d], k), "t", d, i)

    def t_forward(d, i):
        u = 3 * d + (1 - 2 * d) * i
        return hop(t_rows(t_block[d], u), t_rows(3, u), dev(x, y, zn[d], k), "tf", d, i)

    def t_sibling(block, u):
        return hop(t_rows(block, u), t_rows(block, u), dev(x, y, z, 1 - k), "ts", block, u)

    def t_start(i):
        for d in range(2):
            go(t_copy(d, i))

    def t_step(i):
        for d in range(2):
            t_copy(d, i).wait_recv()
            if i < 2:
                go(t_forward(d, i))
            go(t_sibling(t_block[d], 3 * d + (1 - 2 * d) * i))

    def t_last(i):
        for d in range(2):
            t_forward(d, i).wait_recv()
            go(t_sibling(3, 3 * d + (1 - 2 * d) * i))

    def slab_place(block):
        rows = pl.ds(pl.multiple_of(y * 16, 16), 16)
        return a_mat.at[:, rows, pl.ds(pl.multiple_of(block * 128, 128), 128)]

    slab_rows = a_mat.at[:, pl.ds(pl.multiple_of(y * 16, 16), 16), :]

    def slab_y(d, s):
        slot = lax.rem(y + (NY - s if d == 0 else s), NY)
        part = a_mat.at[:, pl.ds(pl.multiple_of(slot * 16, 16), 16), :]
        return hop(part, part, dev(x, ys[d], z, k), "b", d, s)

    def v0_y(d, s):
        slot = s0.at[lax.rem(y + (NY - s if d == 0 else s), NY)]
        return hop(slot, slot, dev(x, ys[d], z, k), "v0y", d, s)

    def v0_rows(slot, part):
        return v_all.at[pl.ds(pl.multiple_of(slot * 64 + part * 16, 16), 16)]

    def v0_x(d, part):
        rows = v0_rows(x, part)
        return hop(rows, rows, dev(xs[d], y, z, k), "v0x", d, part)

    def v0_f(d):
        rows = v0_rows(xs[1 - d], d)
        return hop(rows, rows, dev(xs[d], y, z, k), "v0f", d)

    def v1_x(n):
        slot = x1.at[x]
        return hop(slot, slot, dev(lax.rem(x + n, NX), y, z, k), "v1x", n)

    def v1_y(d, s, e):
        lanes = pl.ds(1408 * e, 1408 - 128 * e)
        slot = s1.at[lax.rem(y + (NY - s if d == 0 else s), NY), :, lanes]
        return hop(slot, slot, dev(x, ys[d], z, k), "v1y", d, s, e)

    there = pick(v * 4 + zl, PLACE_OF)
    moves = there != z * 2 + k
    go_there = dev(x, y, lax.div(there, 2), lax.rem(there, 2))
    raw = [
        (v_own.at[pl.ds(0, 32)], s0.at[y], sem("r", 0)),
        (v_own.at[pl.ds(32, 32)], x1.at[x], sem("r", 1)),
    ]

    @pl.when(moves)
    def _():
        for src, dst, n in raw:
            remote(src, dst, ssem.at[n], rsem.at[n], go_there).start()

    @pl.when(jnp.logical_not(moves))
    def _():
        for src, dst, n in raw:
            pltpu.make_async_copy(src, dst, rsem.at[n]).start()

    for b in range(4):
        at = pick(v * 4 + b, PLACE_OF)
        az, ak = lax.div(at, 2), lax.rem(at, 2)
        above = lax.rem(zl - lax.rem(az, NZL) + NZL, NZL)
        block = jnp.where(above == 0, 0, jnp.where(above == 3, 1, above + 1))
        mine = at == z * 2 + k

        @pl.when(mine)
        def _():
            pltpu.make_async_copy(a_own, slab_place(0), a_recv).start()

        @pl.when(jnp.logical_not(mine))
        def _():
            remote(a_own, slab_place(block), a_send, a_recv, dev(x, y, az, ak)).start()

    t_start(0)
    t_start(1)
    for src, dst, n in raw:
        pltpu.make_async_copy(src, dst, rsem.at[n]).wait()
        if n == raw[0][2]:
            go(v0_y(0, 0))
            go(v0_y(1, 0))
    for n in range(1, NX):
        go(v1_x(n))

    def v0_step(s):
        v0_y(0, s).wait_recv()
        if s < 3:
            go(v0_y(0, s + 1))
            v0_y(1, s).wait_recv()
        if s < 2:
            go(v0_y(1, s + 1))

    def v1_step(s):
        for e in range(2):
            for d in range(2):
                if s == 3 and d != e:
                    continue
                v1_y(d, s, e).wait_recv()
                if s < 2 or (s == 2 and d == e):
                    go(v1_y(d, s + 1, e))

    def slab_step(s):
        for d in range(2):
            if s == 3 and d == 1:
                continue
            slab_y(d, s).wait_recv()
            if s < 3 - d:
                go(slab_y(d, s + 1))

    def join(source, rows, half):
        for c in range(CW):
            joined = jnp.concatenate([source(half * 4 + q, c) for q in range(4)], axis=1)
            v_all[rows, pl.ds(pl.multiple_of(c * NV + half * 896, 128), 896)] = joined

    def join0(half):
        rows = pl.ds(pl.multiple_of(x * 64, 32), 32)
        join(lambda q, c: s0[q, :, c * 256 : c * 256 + DW], rows, half)

    def join1(half):
        for slot in range(NX):
            first_lane = slot * CW * DW
            join(
                lambda q, c: s1[q, :, first_lane + c * DW : first_lane + c * DW + DW],
                pl.ds(slot * 64 + 32, 32),
                half,
            )

    near_half = lax.div(y, 4)

    def ladder(pair, half):
        for c in range(CW):
            ks = pl.ds(pl.multiple_of(c * NV + half * 896, 128), 896)
            both = dot(t_all[pl.ds(pair * 16, 16), :, ks].reshape(256, 896), v_all[:, ks], NT)
            for h in range(2):
                acc[h, pl.ds(pair * 256, 256), :] += both[:, h * 128 : h * 128 + 128]

    v0_step(0)
    for n in range(1, NX):
        v1_x(n).wait_recv()
    s1[y] = jnp.concatenate(
        [x1[slot, :, c * 256 : c * 256 + DW] for slot in range(NX) for c in range(CW)], axis=1
    )
    for e in range(2):
        go(v1_y(0, 0, e))
        go(v1_y(1, 0, e))
    v0_step(1)
    pltpu.make_async_copy(slab_rows, slab_rows, a_recv).wait()
    go(slab_y(0, 0))
    go(slab_y(1, 0))
    v0_step(2)
    t_step(0)
    t_start(2)
    v1_step(0)
    t_step(1)
    t_start(3)
    v0_step(3)
    for half in range(2):
        join0(half)
    go(v0_x(0, 0))
    go(v0_x(1, 1))
    go(v0_x(0, 1))
    go(v0_x(1, 0))
    slab_step(0)
    m = lax.broadcasted_iota(jnp.int32, (256, 256), 0)
    n = lax.broadcasted_iota(jnp.int32, (256, 256), 1)
    hit = jnp.logical_and(m >> 4 == (n & 15), (m & 15) == n >> 4)
    swap[...] = jnp.where(hit, 1.0, 0.0).astype(jnp.bfloat16)
    lane = lax.broadcasted_iota(jnp.int32, (16, 256), 1)
    line = lax.broadcasted_iota(jnp.int32, (16, 256), 0)
    e_j = jnp.zeros((16, 256), jnp.float32)
    e_a = jnp.zeros((16, 256), jnp.float32)
    e_b = jnp.zeros((16, 256), jnp.float32)
    for n in range(16):
        e_j = jnp.where(line == n, occ[y * 16 + n], e_j)
        e_a = jnp.where(lane >> 4 == n, vir[blk_a * 16 + n], e_a)
        e_b = jnp.where((lane & 15) == n, vir[blk_b * 16 + n], e_b)
    for block in range(4):
        for q in range(8):
            e_i = occ[q * 16 + lax.rem(zl + ABOVE[block], NZL) * 4 + x]
            denom[block * 128 + q * 16 : block * 128 + q * 16 + 16, :] = ((e_i + e_j) - e_a) - e_b
    v1_step(1)
    slab_step(1)
    m = lax.broadcasted_iota(jnp.int32, (512, 512), 0)
    n = lax.broadcasted_iota(jnp.int32, (512, 512), 1)
    hit = jnp.logical_and((m >> 4 & 7) == n >> 6, m >> 7 == (n >> 4 & 3))
    hit = jnp.logical_and(hit, (m & 15) == (n & 15))
    order[...] = jnp.where(hit, 1.0, 0.0).astype(jnp.bfloat16)

    v0_x(0, 0).wait_recv()
    go(v0_f(0))
    v0_x(1, 1).wait_recv()
    go(v0_f(1))
    slab_step(2)
    t_step(2)
    v1_step(2)
    slab_step(3)
    w_load.wait()
    zmat = None
    for c in range(CW):
        rows = w_own[:, c, pl.ds(pl.multiple_of(blk_b * 16, 16), 16), :].reshape(256, NO)
        part = dot(rows, a_mat[c])
        zmat = part if zmat is None else zmat + part
    for block in range(4):
        zs[block] = zmat[:, block * 128 : block * 128 + 128]
    chunk = lax.broadcasted_iota(jnp.int32, (16, 128), 1) >> 4

    def crossed(block, carry):
        for h in range(2):
            outs = [jnp.zeros((16, 128), jnp.float32)] * 8
            for b in range(8):
                part = zs[block, pl.ds(h * 8 + b, 16, stride=16), :]
                for q in range(8):
                    moved = pltpu.roll(part, (b - q) % 8 * 16, 1) if b != q else part
                    outs[q] = jnp.where(chunk == b, -moved, outs[q])
            for q in range(8):
                acc[h, pl.ds(pl.multiple_of(block * 128 + q * 16, 16), 16), :] = outs[q]
        return carry

    lax.fori_loop(0, 4, crossed, 0)

    t_step(3)
    t_last(0)
    v0_x(0, 1).wait_recv()
    v0_x(1, 0).wait_recv()
    for d in range(2):
        v0_f(d).wait_recv()
    join1(near_half)
    for u in range(4):
        t_sibling(1, u).wait_recv()
    ladder(0, near_half)
    v1_step(3)
    join1(1 - near_half)
    def near(n):
        return lax.rem(zl + ABOVE[n], NZL)

    def tile_row(si, sj, h):
        return (si // 2 * 2 + sj // 2) * 8 + (si % 2 * 2 + sj % 2) * 2 + h

    def fill(pair, half):
        for si in (2 * pair, 2 * pair + 1):
            for sj in (2 * half, 2 * half + 1):
                for xj in range(4):
                    for h in range(2):
                        mail[pl.ds(xj * 256 + tile_row(si, sj, h), 8, stride=32), :] = acc[
                            h, pl.ds(si * 128 + near(sj) * 4 + xj, 8, stride=16), :
                        ]

    def post(part, start, rows):
        def send_mail(n, carry):
            px, py = partner(n)
            src = mail.at[pl.ds(pl.multiple_of((px * 8 + py) * 32 + start, 8), rows)]
            dst = rec.at[pl.ds(pl.multiple_of((x * 8 + y) * 32 + start, 8), rows)]
            remote(src, dst, m_send.at[part], m_recv.at[part], dev(px, py, z, twin)).start()
            return carry

        lax.fori_loop(0, 32 - first, send_mail, 0)

        @pl.when(diag)
        def _():
            here = pl.ds(pl.multiple_of((x * 8 + y) * 32 + start, 8), rows)
            pltpu.make_async_copy(mail.at[here], rec.at[here], m_recv.at[part]).start()

    ladder(0, 1 - near_half)
    fill(0, 0)
    fill(0, 1)
    post(0, 0, 16)
    t_last(1)
    for block in (2, 3):
        for u in range(4):
            t_sibling(block, u).wait_recv()
    for half in range(2):
        ladder(1, half)
    fill(1, 0)
    post(1, 16, 8)
    fill(1, 1)
    post(2, 24, 8)

    owner_z = lax.div(blk_a, 2) * NZL
    owner_k = lax.rem(blk_a, 2)
    for block in range(4):
        rows = pl.ds(block * 128, 128)
        turned = None
        for h in range(2):
            part = acc[h, rows, :]
            hi = part.astype(jnp.bfloat16)
            rest = part - hi.astype(jnp.float32)
            mid = rest.astype(jnp.bfloat16)
            low = (rest - mid.astype(jnp.float32)).astype(jnp.bfloat16)
            matrix = swap[h * 128 : h * 128 + 128, :]
            term = dot(hi, matrix) + (dot(mid, matrix) + dot(low, matrix))
            turned = term if turned is None else turned + term
        for h in range(2):
            own_x[h, rows, :] = turned[:, h * 128 : h * 128 + 128]

    def arrived(part, count):
        some = rec.at[pl.ds(0, count)]
        pltpu.make_async_copy(some, some, m_recv.at[part]).wait()

    def take(pair, half):
        for si in (2 * pair, 2 * pair + 1):
            for sj in (2 * half, 2 * half + 1):
                for xj in range(4):
                    for h in range(2):
                        rows = pl.ds(sj * 128 + near(si) * 4 + xj, 8, stride=16)
                        own_x[h, rows, :] += rec[pl.ds(xj * 256 + tile_row(si, sj, h), 8, stride=32), :]

    arrived(0, 512)
    take(0, 0)
    take(0, 1)
    for half in range(2):
        arrived(1 + half, 256)
        take(1, half)
        for sj in (2 * half, 2 * half + 1):
            rows = pl.ds(sj * 128, 128)
            for h in range(2):
                lanes = pl.ds(h * 128, 128)
                sbuf[rows, lanes] = (own_x[h, rows, :] / denom[rows, lanes]).astype(jnp.bfloat16)
            target = owner_z + near(sj)
            n = sem("d", sj)
            if sj == 0:

                @pl.when(own)
                def _():
                    pltpu.make_async_copy(sbuf.at[rows], d_all.at[blk_b], d_recv.at[blk_b]).start()

                @pl.when(jnp.logical_not(own))
                def _():
                    remote(sbuf.at[rows], d_all.at[blk_b], ssem.at[n], d_recv.at[blk_b], dev(x, y, target, owner_k)).start()
            else:
                go(remote(sbuf.at[rows], d_all.at[blk_b], ssem.at[n], d_recv.at[blk_b], dev(x, y, target, owner_k)))

    parts = [None, None]
    for b in range(4):
        pltpu.make_async_copy(d_all.at[b], d_all.at[b], d_recv.at[b]).wait()
        for h in range(2):
            term = dot(d_all[b, :, h * 128 : h * 128 + 128], order[b * 128 : b * 128 + 128, :])
            parts[h] = term if b == 0 else parts[h] + term
    for h in range(2):
        out_ref[:, h * 512 : h * 512 + 512] = parts[h].astype(jnp.bfloat16)

    for copy in sends:
        copy.wait_send()

    @pl.when(moves)
    def _():
        for src, dst, n in raw:
            pltpu.make_async_copy(src, src, ssem.at[n]).wait()

    @pl.when(jnp.logical_not(own))
    def _():
        some = sbuf.at[pl.ds(0, 128)]
        pltpu.make_async_copy(some, some, ssem.at[sem("d", 0)]).wait()

    three = a_mat.at[:, pl.ds(0, 16), pl.ds(0, 384)]

    @pl.when(own)
    def _():
        pltpu.make_async_copy(three, three, a_send).wait()

    @pl.when(jnp.logical_not(own))
    def _():
        pltpu.make_async_copy(slab_rows, slab_rows, a_send).wait()

    for part, rows in ((0, 16), (1, 8), (2, 8)):

        @pl.when(diag)
        def _():
            some = rec.at[pl.ds(0, 31 * rows)]
            pltpu.make_async_copy(some, some, m_send.at[part]).wait()

        @pl.when(jnp.logical_not(diag))
        def _():
            some = rec.at[pl.ds(0, 32 * rows)]
            pltpu.make_async_copy(some, some, m_send.at[part]).wait()


def call(t, vv, w, irreps, occ, vir):
    bf, f32 = jnp.bfloat16, jnp.float32
    vm = pl.BlockSpec(memory_space=pltpu.VMEM)
    smem = pl.BlockSpec(memory_space=pltpu.SMEM)
    anywhere = pl.BlockSpec(memory_space=pl.ANY)
    dma = pltpu.SemaphoreType.DMA
    return pl.pallas_call(
        kernel,
        out_shape=jax.ShapeDtypeStruct((NO, 1024), bf),
        in_specs=[anywhere, anywhere, anywhere, smem, smem, smem],
        out_specs=vm,
        scratch_shapes=[
            pltpu.VMEM((32, 16, KK), bf),
            pltpu.VMEM((NY, 32, PIECE), bf),
            pltpu.VMEM((NX, 32, PIECE), bf),
            pltpu.VMEM((NY, 32, NX * CW * DW), bf),
            pltpu.VMEM((256, KK), bf),
            pltpu.VMEM((CW, NO, 512), bf),
            pltpu.VMEM((4, 256, 128), f32),
            pltpu.VMEM((2, 512, 128), f32),
            pltpu.VMEM((2, 512, 128), f32),
            pltpu.VMEM((512, 512), bf),
            pltpu.VMEM((256, 256), bf),
            pltpu.VMEM((1024, 128), bf),
            pltpu.VMEM((CW, 16, 128), bf),
            pltpu.VMEM((16, CW, 4, DW), bf),
            pltpu.VMEM((64, PIECE), bf),
            pltpu.VMEM((16, CW, SA, NO), bf),
            pltpu.VMEM((512, 256), f32),
            pltpu.VMEM((1024, 128), f32),
            pltpu.VMEM((1024, 128), f32),
            pltpu.VMEM((512, 256), bf),
            pltpu.VMEM((4, 128, 256), bf),
            dma((96,)), dma((96,)), dma((5,)), dma, dma, dma((3,)), dma((3,)), dma((4,)),
        ],
        compiler_params=pltpu.CompilerParams(
            collective_id=0, has_side_effects=True, vmem_limit_bytes=64 * 1024 * 1024
        ),
        cost_estimate=pl.CostEstimate(flops=2 * 512 * 256 * KK, bytes_accessed=20_000_000, transcendentals=0),
    )(t, vv, w, irreps, occ, vir)


def local(amplitudes, integrals, hole_integrals, irreps, occ_energy, vir_energy):
    t = jnp.transpose(amplitudes.reshape(8, 16, CW, NV), (0, 2, 1, 3))
    vv = jnp.transpose(integrals, (0, 2, 1, 3))
    w = jnp.transpose(hole_integrals.reshape(NO, 16, CW, SA), (1, 2, 3, 0))
    out = call(t, vv, w, irreps, occ_energy, vir_energy)
    return out.reshape(8, 1, 1, 1, 16, 16, SA)


def solution(mesh):
    in_specs = (
        P(None, "row", None, "col", None, None, None),
        P("vir", "row", None, "col"),
        P(None, None, "col", None, None, None),
        P(),
        P(),
        P(),
    )
    out_specs = P(None, "row", None, "col", None, "vir", None)
    return jax.shard_map(local, mesh=mesh, in_specs=in_specs, out_specs=out_specs, check_vma=False)
```

```python
import jax
import jax.numpy as jnp
from jax import lax
from jax.experimental import pallas as pl
from jax.experimental.pallas import tpu as pltpu
from jax.sharding import PartitionSpec as P

NO = 128
NV = 1792
SA = 64
CW = 3
VBLK = 16
KK = CW * NV
NX, NY, NZ, NZL = 4, 8, 8, 4
DW = NV // NY
PIECE = CW * 256
MESH = pl.DeviceIdType.MESH
NT = (((1,), (1,)), ((), ()))
NN = (((1,), (0,)), ((), ()))

WORK = [
    (0, 1), (1, 0), (0, 0), (1, 1), (2, 1), (1, 2), (0, 3), (3, 0),
    (2, 0), (0, 2), (1, 3), (3, 1), (2, 2), (3, 3), (2, 3), (3, 2),
]
ABOVE = (0, 3, 1, 2)
PLACE_OF = [WORK.index((a, b)) for a in range(4) for b in range(4)]


def pick(index, table):
    value = jnp.int32(table[0])
    for n in range(1, len(table)):
        value = jnp.where(index == n, jnp.int32(table[n]), value)
    return value


def dev(x, y, z, k):
    return (lax.rem(z, NZL) * NX + x, y, lax.div(z, NZL) * 2 + k)


def dot(a, b, dims=NN):
    return lax.dot_general(a, b, dims, preferred_element_type=jnp.float32)


def remote(src, dst, send, recv, where):
    return pltpu.make_async_remote_copy(
        src_ref=src, dst_ref=dst, send_sem=send, recv_sem=recv, device_id=where, device_id_type=MESH
    )


def kernel(
    t_ref, v_ref, w_ref, irreps, occ, vir, out_ref,
    t_all, s0, x1, s1, v_all, a_mat, zs, acc, own_x, order, swap, pull, a_own, v_raw, v_own, w_own, denom, mail, rec, sbuf, d_all,
    ssem, rsem, load_sem, a_send, a_recv, m_send, m_recv, d_recv,
):
    r = lax.axis_index("row")
    y = lax.axis_index("col")
    v = lax.axis_index("vir")
    x, zl = lax.rem(r, NX), lax.div(r, NX)
    zh, k = lax.div(v, 2), lax.rem(v, 2)
    z = zh * NZL + zl
    xs = (lax.rem(x + 1, NX), lax.rem(x + NX - 1, NX))
    ys = (lax.rem(y + 1, NY), lax.rem(y + NY - 1, NY))
    zn = (lax.rem(z + 1, NZ), lax.rem(z + NZ - 1, NZ))
    blk_a = pick(z * 2 + k, [w[0] for w in WORK])
    blk_b = pick(z * 2 + k, [w[1] for w in WORK])
    diag = blk_a == blk_b
    own = blk_a == v
    twin = jnp.where(diag, k, 1 - k)

    t_loads = [
        pltpu.make_async_copy(
            t_ref.at[:, c], t_all.at[pl.ds(0, 8), :, pl.ds(c * NV, NV)], load_sem.at[c]
        )
        for c in range(CW)
    ]
    w_load = pltpu.make_async_copy(w_ref, w_own, load_sem.at[3])
    for load in t_loads:
        load.start()
    w_load.start()
    v_load = pltpu.make_async_copy(v_ref, v_raw, load_sem.at[4])
    v_load.start()

    barrier = pltpu.get_barrier_semaphore()

    def greet(where):
        pl.semaphore_signal(barrier, inc=1, device_id=where, device_id_type=MESH)

    for n in range(1, NX):
        greet(dev(lax.rem(x + n, NX), y, z, k))

    for d in range(2):
        greet(dev(x, ys[d], z, k))

    def greet_z(n, carry):
        other = lax.rem(z * 2 + k + n, 16)
        greet(dev(x, y, lax.div(other, 2), lax.rem(other, 2)))
        return carry

    lax.fori_loop(1, 16, greet_z, 0)
    first = jnp.where(diag, 1, 0)

    def partner(n):
        m = lax.div(n, NX)
        far = jnp.where(lax.rem(m, 2) == 1, 4 - lax.div(m + 1, 2), 4 + lax.div(m, 2))
        return (lax.rem(x + 3 - lax.rem(n, NX), NX), lax.rem(y + far, NY))

    label = jnp.bitwise_xor(jnp.bitwise_xor(irreps[v], irreps[zl]), irreps[0])
    lane = lax.broadcasted_iota(jnp.int32, (8, PIECE), 1) & 255
    kept = jnp.zeros((8, PIECE), jnp.float32)
    for n in range(DW // VBLK):
        same = jnp.where(irreps[y * (DW // VBLK) + n] == label, 1.0, 0.0)
        kept = jnp.where(lane >> 4 == n, same, kept)
    v_own[...] = jnp.zeros_like(v_own)
    v_load.wait()
    for b in range(4):
        for c in range(CW):
            part = v_raw[:, c, b, :].astype(jnp.float32) * kept[0:1, :DW]
            v_own[b * 16 : b * 16 + 16, c * 256 : c * 256 + DW] = part.astype(jnp.bfloat16)

    m = lax.broadcasted_iota(jnp.int32, (1024, 128), 0)
    n = lax.broadcasted_iota(jnp.int32, (1024, 128), 1)
    hit = jnp.logical_and(m >> 7 == n >> 4, (m & 127) == (n & 15) + v * 16)
    pull[...] = jnp.where(hit, 1.0, 0.0).astype(jnp.bfloat16)
    for load in t_loads:
        load.wait()
    wide = jnp.concatenate(
        [
            jnp.concatenate([t_all[q, :, c * NV : c * NV + 128] for q in range(8)], axis=1)
            for c in range(CW)
        ],
        axis=0,
    )
    a_own[...] = dot(wide, pull[...]).astype(jnp.bfloat16).reshape(CW, 16, 128)
    pl.semaphore_wait(barrier, 3 + 2 + 15)

    names = {}
    sends = []

    def sem(*name):
        return names.setdefault(name, len(names))

    def hop(src, dst, where, *name):
        n = sem(*name)
        return remote(src, dst, ssem.at[n], rsem.at[n], where)

    def go(copy):
        copy.start()
        sends.append(copy)

    t_block = (1, 2)

    def t_rows(block, u):
        return t_all.at[pl.ds(block * 8 + k * 4 + u, 1)]

    def t_copy(d, i):
        u = 3 * d + (1 - 2 * d) * i
        return hop(t_rows(0, u), t_rows(t_block[d], u), dev(x, y, zn[d], k), "t", d, i)

    def t_forward(d, i):
        u = 3 * d + (1 - 2 * d) * i
        return hop(t_rows(t_block[d], u), t_rows(3, u), dev(x, y, zn[d], k), "tf", d, i)

    def t_sibling(block, u):
        return hop(t_rows(block, u), t_rows(block, u), dev(x, y, z, 1 - k), "ts", block, u)

    def t_start(i):
        for d in range(2):
            go(t_copy(d, i))

    def t_step(i):
        for d in range(2):
            t_copy(d, i).wait_recv()
            if i < 2:
                go(t_forward(d, i))
            go(t_sibling(t_block[d], 3 * d + (1 - 2 * d) * i))

    def t_last(i):
        for d in range(2):
            t_forward(d, i).wait_recv()
            go(t_sibling(3, 3 * d + (1 - 2 * d) * i))

    def slab_place(block):
        rows = pl.ds(pl.multiple_of(y * 16, 16), 16)
        return a_mat.at[:, rows, pl.ds(pl.multiple_of(block * 128, 128), 128)]

    slab_rows = a_mat.at[:, pl.ds(pl.multiple_of(y * 16, 16), 16), :]

    def slab_y(d, s):
        slot = lax.rem(y + (NY - s if d == 0 else s), NY)
        part = a_mat.at[:, pl.ds(pl.multiple_of(slot * 16, 16), 16), :]
        return hop(part, part, dev(x, ys[d], z, k), "b", d, s)

    def v0_y(d, s):
        slot = s0.at[lax.rem(y + (NY - s if d == 0 else s), NY)]
        return hop(slot, slot, dev(x, ys[d], z, k), "v0y", d, s)

    def v0_rows(slot, part):
        return v_all.at[pl.ds(pl.multiple_of(slot * 64 + part * 16, 16), 16)]

    def v0_x(d, part):
        rows = v0_rows(x, part)
        return hop(rows, rows, dev(xs[d], y, z, k), "v0x", d, part)

    def v0_f(d):
        rows = v0_rows(xs[1 - d], d)
        return hop(rows, rows, dev(xs[d], y, z, k), "v0f", d)

    def v1_x(n):
        slot = x1.at[x]
        return hop(slot, slot, dev(lax.rem(x + n, NX), y, z, k), "v1x", n)

    def v1_y(d, s, e):
        lanes = pl.ds(1408 * e, 1408 - 128 * e)
        slot = s1.at[lax.rem(y + (NY - s if d == 0 else s), NY), :, lanes]
        return hop(slot, slot, dev(x, ys[d], z, k), "v1y", d, s, e)

    there = pick(v * 4 + zl, PLACE_OF)
    moves = there != z * 2 + k
    go_there = dev(x, y, lax.div(there, 2), lax.rem(there, 2))
    raw = [
        (v_own.at[pl.ds(0, 32)], s0.at[y], sem("r", 0)),
        (v_own.at[pl.ds(32, 32)], x1.at[x], sem("r", 1)),
    ]

    @pl.when(moves)
    def _():
        for src, dst, n in raw:
            remote(src, dst, ssem.at[n], rsem.at[n], go_there).start()

    @pl.when(jnp.logical_not(moves))
    def _():
        for src, dst, n in raw:
            pltpu.make_async_copy(src, dst, rsem.at[n]).start()

    for b in range(4):
        at = pick(v * 4 + b, PLACE_OF)
        az, ak = lax.div(at, 2), lax.rem(at, 2)
        above = lax.rem(zl - lax.rem(az, NZL) + NZL, NZL)
        block = jnp.where(above == 0, 0, jnp.where(above == 3, 1, above + 1))
        mine = at == z * 2 + k

        @pl.when(mine)
        def _():
            pltpu.make_async_copy(a_own, slab_place(0), a_recv).start()

        @pl.when(jnp.logical_not(mine))
        def _():
            remote(a_own, slab_place(block), a_send, a_recv, dev(x, y, az, ak)).start()

    for src, dst, n in raw:
        pltpu.make_async_copy(src, dst, rsem.at[n]).wait()
        if n == raw[0][2]:
            go(v0_y(0, 0))
            go(v0_y(1, 0))
    for n in range(1, NX):
        go(v1_x(n))
    t_start(0)
    t_start(1)

    def v0_step(s):
        v0_y(0, s).wait_recv()
        if s < 3:
            go(v0_y(0, s + 1))
            v0_y(1, s).wait_recv()
        if s < 2:
            go(v0_y(1, s + 1))

    def v1_step(s):
        for e in range(2):
            for d in range(2):
                if s == 3 and d != e:
                    continue
                v1_y(d, s, e).wait_recv()
                if s < 2 or (s == 2 and d == e):
                    go(v1_y(d, s + 1, e))

    def slab_step(s):
        for d in range(2):
            if s == 3 and d == 1:
                continue
            slab_y(d, s).wait_recv()
            if s < 3 - d:
                go(slab_y(d, s + 1))

    def join(source, rows, half):
        for c in range(CW):
            joined = jnp.concatenate([source(half * 4 + q, c) for q in range(4)], axis=1)
            v_all[rows, pl.ds(pl.multiple_of(c * NV + half * 896, 128), 896)] = joined

    def join0(half):
        rows = pl.ds(pl.multiple_of(x * 64, 32), 32)
        join(lambda q, c: s0[q, :, c * 256 : c * 256 + DW], rows, half)

    def join1(half):
        for slot in range(NX):
            first_lane = slot * CW * DW
            join(
                lambda q, c: s1[q, :, first_lane + c * DW : first_lane + c * DW + DW],
                pl.ds(slot * 64 + 32, 32),
                half,
            )

    near_half = lax.div(y, 4)

    def ladder(pair, half):
        for c in range(CW):
            ks = pl.ds(pl.multiple_of(c * NV + half * 896, 128), 896)
            both = dot(t_all[pl.ds(pair * 16, 16), :, ks].reshape(256, 896), v_all[:, ks], NT)
            for h in range(2):
                acc[h, pl.ds(pair * 256, 256), :] += both[:, h * 128 : h * 128 + 128]

    v0_step(0)
    for n in range(1, NX):
        v1_x(n).wait_recv()
    s1[y] = jnp.concatenate(
        [x1[slot, :, c * 256 : c * 256 + DW] for slot in range(NX) for c in range(CW)], axis=1
    )
    for e in range(2):
        go(v1_y(0, 0, e))
        go(v1_y(1, 0, e))
    v0_step(1)
    pltpu.make_async_copy(slab_rows, slab_rows, a_recv).wait()
    go(slab_y(0, 0))
    go(slab_y(1, 0))
    v0_step(2)
    t_step(0)
    t_start(2)
    v1_step(0)
    t_step(1)
    t_start(3)
    v0_step(3)
    for half in range(2):
        join0(half)
    go(v0_x(0, 0))
    go(v0_x(1, 1))
    go(v0_x(0, 1))
    go(v0_x(1, 0))
    slab_step(0)
    v1_step(1)
    slab_step(1)
    v0_x(0, 0).wait_recv()
    go(v0_f(0))
    v0_x(1, 1).wait_recv()
    go(v0_f(1))
    slab_step(2)
    t_step(2)
    v1_step(2)
    slab_step(3)
    w_load.wait()
    zmat = None
    for c in range(CW):
        rows = w_own[:, c, pl.ds(pl.multiple_of(blk_b * 16, 16), 16), :].reshape(256, NO)
        part = dot(rows, a_mat[c])
        zmat = part if zmat is None else zmat + part
    for block in range(4):
        zs[block] = zmat[:, block * 128 : block * 128 + 128]
    chunk = lax.broadcasted_iota(jnp.int32, (16, 128), 1) >> 4

    def crossed(block, carry):
        for h in range(2):
            outs = [jnp.zeros((16, 128), jnp.float32)] * 8
            for b in range(8):
                part = zs[block, pl.ds(h * 8 + b, 16, stride=16), :]
                for q in range(8):
                    moved = pltpu.roll(part, (b - q) % 8 * 16, 1) if b != q else part
                    outs[q] = jnp.where(chunk == b, -moved, outs[q])
            for q in range(8):
                acc[h, pl.ds(pl.multiple_of(block * 128 + q * 16, 16), 16), :] = outs[q]
        return carry

    lax.fori_loop(0, 4, crossed, 0)

    t_step(3)
    t_last(0)
    v0_x(0, 1).wait_recv()
    v0_x(1, 0).wait_recv()
    for d in range(2):
        v0_f(d).wait_recv()
    join1(near_half)
    for u in range(4):
        t_sibling(1, u).wait_recv()
    ladder(0, near_half)
    v1_step(3)
    join1(1 - near_half)
    def near(n):
        return lax.rem(zl + ABOVE[n], NZL)

    def tile_row(si, sj, h):
        return (si // 2 * 2 + sj // 2) * 8 + (si % 2 * 2 + sj % 2) * 2 + h

    def fill(pair, half):
        for si in (2 * pair, 2 * pair + 1):
            for sj in (2 * half, 2 * half + 1):
                for xj in range(4):
                    for h in range(2):
                        mail[pl.ds(xj * 256 + tile_row(si, sj, h), 8, stride=32), :] = acc[
                            h, pl.ds(si * 128 + near(sj) * 4 + xj, 8, stride=16), :
                        ]

    def post(part, start, rows):
        def send_mail(n, carry):
            px, py = partner(n)
            src = mail.at[pl.ds(pl.multiple_of((px * 8 + py) * 32 + start, 8), rows)]
            dst = rec.at[pl.ds(pl.multiple_of((x * 8 + y) * 32 + start, 8), rows)]
            remote(src, dst, m_send.at[part], m_recv.at[part], dev(px, py, z, twin)).start()
            return carry

        lax.fori_loop(0, 32 - first, send_mail, 0)

        @pl.when(diag)
        def _():
            here = pl.ds(pl.multiple_of((x * 8 + y) * 32 + start, 8), rows)
            pltpu.make_async_copy(mail.at[here], rec.at[here], m_recv.at[part]).start()

    ladder(0, 1 - near_half)
    fill(0, 0)
    fill(0, 1)
    post(0, 0, 16)
    t_last(1)
    for block in (2, 3):
        for u in range(4):
            t_sibling(block, u).wait_recv()
    for half in range(2):
        ladder(1, half)
    fill(1, 0)
    post(1, 16, 8)
    fill(1, 1)
    post(2, 24, 8)

    m = lax.broadcasted_iota(jnp.int32, (256, 256), 0)
    n = lax.broadcasted_iota(jnp.int32, (256, 256), 1)
    hit = jnp.logical_and(m >> 4 == (n & 15), (m & 15) == n >> 4)
    swap[...] = jnp.where(hit, 1.0, 0.0).astype(jnp.bfloat16)
    lane = lax.broadcasted_iota(jnp.int32, (16, 256), 1)
    line = lax.broadcasted_iota(jnp.int32, (16, 256), 0)
    e_j = jnp.zeros((16, 256), jnp.float32)
    e_a = jnp.zeros((16, 256), jnp.float32)
    e_b = jnp.zeros((16, 256), jnp.float32)
    for n in range(16):
        e_j = jnp.where(line == n, occ[y * 16 + n], e_j)
        e_a = jnp.where(lane >> 4 == n, vir[blk_a * 16 + n], e_a)
        e_b = jnp.where((lane & 15) == n, vir[blk_b * 16 + n], e_b)
    for block in range(4):
        for q in range(8):
            e_i = occ[q * 16 + lax.rem(zl + ABOVE[block], NZL) * 4 + x]
            denom[block * 128 + q * 16 : block * 128 + q * 16 + 16, :] = ((e_i + e_j) - e_a) - e_b
    m = lax.broadcasted_iota(jnp.int32, (512, 512), 0)
    n = lax.broadcasted_iota(jnp.int32, (512, 512), 1)
    hit = jnp.logical_and((m >> 4 & 7) == n >> 6, m >> 7 == (n >> 4 & 3))
    hit = jnp.logical_and(hit, (m & 15) == (n & 15))
    order[...] = jnp.where(hit, 1.0, 0.0).astype(jnp.bfloat16)

    owner_z = lax.div(blk_a, 2) * NZL
    owner_k = lax.rem(blk_a, 2)
    for block in range(4):
        rows = pl.ds(block * 128, 128)
        turned = None
        for h in range(2):
            part = acc[h, rows, :]
            hi = part.astype(jnp.bfloat16)
            rest = part - hi.astype(jnp.float32)
            mid = rest.astype(jnp.bfloat16)
            low = (rest - mid.astype(jnp.float32)).astype(jnp.bfloat16)
            matrix = swap[h * 128 : h * 128 + 128, :]
            term = dot(hi, matrix) + (dot(mid, matrix) + dot(low, matrix))
            turned = term if turned is None else turned + term
        for h in range(2):
            own_x[h, rows, :] = turned[:, h * 128 : h * 128 + 128]

    def arrived(part, count):
        some = rec.at[pl.ds(0, count)]
        pltpu.make_async_copy(some, some, m_recv.at[part]).wait()

    def take(pair, half):
        for si in (2 * pair, 2 * pair + 1):
            for sj in (2 * half, 2 * half + 1):
                for xj in range(4):
                    for h in range(2):
                        rows = pl.ds(sj * 128 + near(si) * 4 + xj, 8, stride=16)
                        own_x[h, rows, :] += rec[pl.ds(xj * 256 + tile_row(si, sj, h), 8, stride=32), :]

    arrived(0, 512)
    take(0, 0)
    take(0, 1)
    for half in range(2):
        arrived(1 + half, 256)
        take(1, half)
        for sj in (2 * half, 2 * half + 1):
            rows = pl.ds(sj * 128, 128)
            for h in range(2):
                lanes = pl.ds(h * 128, 128)
                sbuf[rows, lanes] = (own_x[h, rows, :] / denom[rows, lanes]).astype(jnp.bfloat16)
            target = owner_z + near(sj)
            n = sem("d", sj)
            if sj == 0:

                @pl.when(own)
                def _():
                    pltpu.make_async_copy(sbuf.at[rows], d_all.at[blk_b], d_recv.at[blk_b]).start()

                @pl.when(jnp.logical_not(own))
                def _():
                    remote(sbuf.at[rows], d_all.at[blk_b], ssem.at[n], d_recv.at[blk_b], dev(x, y, target, owner_k)).start()
            else:
                go(remote(sbuf.at[rows], d_all.at[blk_b], ssem.at[n], d_recv.at[blk_b], dev(x, y, target, owner_k)))

    parts = [None, None]
    for b in range(4):
        pltpu.make_async_copy(d_all.at[b], d_all.at[b], d_recv.at[b]).wait()
        for h in range(2):
            term = dot(d_all[b, :, h * 128 : h * 128 + 128], order[b * 128 : b * 128 + 128, :])
            parts[h] = term if b == 0 else parts[h] + term
    for h in range(2):
        out_ref[:, h * 512 : h * 512 + 512] = parts[h].astype(jnp.bfloat16)

    for copy in sends:
        copy.wait_send()

    @pl.when(moves)
    def _():
        for src, dst, n in raw:
            pltpu.make_async_copy(src, src, ssem.at[n]).wait()

    @pl.when(jnp.logical_not(own))
    def _():
        some = sbuf.at[pl.ds(0, 128)]
        pltpu.make_async_copy(some, some, ssem.at[sem("d", 0)]).wait()

    three = a_mat.at[:, pl.ds(0, 16), pl.ds(0, 384)]

    @pl.when(own)
    def _():
        pltpu.make_async_copy(three, three, a_send).wait()

    @pl.when(jnp.logical_not(own))
    def _():
        pltpu.make_async_copy(slab_rows, slab_rows, a_send).wait()

    for part, rows in ((0, 16), (1, 8), (2, 8)):

        @pl.when(diag)
        def _():
            some = rec.at[pl.ds(0, 31 * rows)]
            pltpu.make_async_copy(some, some, m_send.at[part]).wait()

        @pl.when(jnp.logical_not(diag))
        def _():
            some = rec.at[pl.ds(0, 32 * rows)]
            pltpu.make_async_copy(some, some, m_send.at[part]).wait()


def call(t, vv, w, irreps, occ, vir):
    bf, f32 = jnp.bfloat16, jnp.float32
    vm = pl.BlockSpec(memory_space=pltpu.VMEM)
    smem = pl.BlockSpec(memory_space=pltpu.SMEM)
    anywhere = pl.BlockSpec(memory_space=pl.ANY)
    dma = pltpu.SemaphoreType.DMA
    return pl.pallas_call(
        kernel,
        out_shape=jax.ShapeDtypeStruct((NO, 1024), bf),
        in_specs=[anywhere, anywhere, anywhere, smem, smem, smem],
        out_specs=vm,
        scratch_shapes=[
            pltpu.VMEM((32, 16, KK), bf),
            pltpu.VMEM((NY, 32, PIECE), bf),
            pltpu.VMEM((NX, 32, PIECE), bf),
            pltpu.VMEM((NY, 32, NX * CW * DW), bf),
            pltpu.VMEM((256, KK), bf),
            pltpu.VMEM((CW, NO, 512), bf),
            pltpu.VMEM((4, 256, 128), f32),
            pltpu.VMEM((2, 512, 128), f32),
            pltpu.VMEM((2, 512, 128), f32),
            pltpu.VMEM((512, 512), bf),
            pltpu.VMEM((256, 256), bf),
            pltpu.VMEM((1024, 128), bf),
            pltpu.VMEM((CW, 16, 128), bf),
            pltpu.VMEM((16, CW, 4, DW), bf),
            pltpu.VMEM((64, PIECE), bf),
            pltpu.VMEM((16, CW, SA, NO), bf),
            pltpu.VMEM((512, 256), f32),
            pltpu.VMEM((1024, 128), f32),
            pltpu.VMEM((1024, 128), f32),
            pltpu.VMEM((512, 256), bf),
            pltpu.VMEM((4, 128, 256), bf),
            dma((96,)), dma((96,)), dma((5,)), dma, dma, dma((3,)), dma((3,)), dma((4,)),
        ],
        compiler_params=pltpu.CompilerParams(
            collective_id=0, has_side_effects=True, vmem_limit_bytes=64 * 1024 * 1024
        ),
        cost_estimate=pl.CostEstimate(flops=2 * 512 * 256 * KK, bytes_accessed=20_000_000, transcendentals=0),
    )(t, vv, w, irreps, occ, vir)


def local(amplitudes, integrals, hole_integrals, irreps, occ_energy, vir_energy):
    t = jnp.transpose(amplitudes.reshape(8, 16, CW, NV), (0, 2, 1, 3))
    vv = jnp.transpose(integrals, (0, 2, 1, 3))
    w = jnp.transpose(hole_integrals.reshape(NO, 16, CW, SA), (1, 2, 3, 0))
    out = call(t, vv, w, irreps, occ_energy, vir_energy)
    return out.reshape(8, 1, 1, 1, 16, 16, SA)


def solution(mesh):
    in_specs = (
        P(None, "row", None, "col", None, None, None),
        P("vir", "row", None, "col"),
        P(None, None, "col", None, None, None),
        P(),
        P(),
        P(),
    )
    out_specs = P(None, "row", None, "col", None, "vir", None)
    return jax.shard_map(local, mesh=mesh, in_specs=in_specs, out_specs=out_specs, check_vma=False)
```

```python
import jax
import jax.numpy as jnp
from jax import lax
from jax.experimental import pallas as pl
from jax.experimental.pallas import tpu as pltpu
from jax.sharding import PartitionSpec as P

NO = 128
NV = 1792
SA = 64
CW = 3
VBLK = 16
KK = CW * NV
NX, NY, NZ, NZL = 4, 8, 8, 4
DW = NV // NY
PIECE = CW * 256
MESH = pl.DeviceIdType.MESH
NT = (((1,), (1,)), ((), ()))
NN = (((1,), (0,)), ((), ()))

WORK = [
    (0, 1), (1, 0), (0, 0), (1, 1), (2, 1), (1, 2), (0, 3), (3, 0),
    (2, 0), (0, 2), (1, 3), (3, 1), (2, 2), (3, 3), (2, 3), (3, 2),
]
ABOVE = (0, 3, 1, 2)
PLACE_OF = [WORK.index((a, b)) for a in range(4) for b in range(4)]


def pick(index, table):
    value = jnp.int32(table[0])
    for n in range(1, len(table)):
        value = jnp.where(index == n, jnp.int32(table[n]), value)
    return value


def dev(x, y, z, k):
    return (lax.rem(z, NZL) * NX + x, y, lax.div(z, NZL) * 2 + k)


def dot(a, b, dims=NN):
    return lax.dot_general(a, b, dims, preferred_element_type=jnp.float32)


def remote(src, dst, send, recv, where):
    return pltpu.make_async_remote_copy(
        src_ref=src, dst_ref=dst, send_sem=send, recv_sem=recv, device_id=where, device_id_type=MESH
    )


def kernel(
    t_ref, v_ref, w_ref, irreps, occ, vir, out_ref,
    t_all, s0, x1, s1, v_all, a_mat, zs, acc, own_x, order, swap, pull, a_own, v_raw, v_own, w_own, denom, mail, rec, sbuf, d_all,
    ssem, rsem, load_sem, a_send, a_recv, m_send, m_recv, d_recv,
):
    r = lax.axis_index("row")
    y = lax.axis_index("col")
    v = lax.axis_index("vir")
    x, zl = lax.rem(r, NX), lax.div(r, NX)
    zh, k = lax.div(v, 2), lax.rem(v, 2)
    z = zh * NZL + zl
    xs = (lax.rem(x + 1, NX), lax.rem(x + NX - 1, NX))
    ys = (lax.rem(y + 1, NY), lax.rem(y + NY - 1, NY))
    zn = (lax.rem(z + 1, NZ), lax.rem(z + NZ - 1, NZ))
    blk_a = pick(z * 2 + k, [w[0] for w in WORK])
    blk_b = pick(z * 2 + k, [w[1] for w in WORK])
    diag = blk_a == blk_b
    own = blk_a == v
    twin = jnp.where(diag, k, 1 - k)

    t_loads = [
        pltpu.make_async_copy(
            t_ref.at[:, c], t_all.at[pl.ds(0, 8), :, pl.ds(c * NV, NV)], load_sem.at[c]
        )
        for c in range(CW)
    ]
    w_load = pltpu.make_async_copy(w_ref, w_own, load_sem.at[3])
    for load in t_loads:
        load.start()
    w_load.start()
    v_load = pltpu.make_async_copy(v_ref, v_raw, load_sem.at[4])
    v_load.start()

    barrier = pltpu.get_barrier_semaphore()

    def greet(where):
        pl.semaphore_signal(barrier, inc=1, device_id=where, device_id_type=MESH)

    for n in range(1, NX):
        greet(dev(lax.rem(x + n, NX), y, z, k))

    for d in range(2):
        greet(dev(x, ys[d], z, k))

    def greet_z(n, carry):
        other = lax.rem(z * 2 + k + n, 16)
        greet(dev(x, y, lax.div(other, 2), lax.rem(other, 2)))
        return carry

    lax.fori_loop(1, 16, greet_z, 0)
    first = jnp.where(diag, 1, 0)

    def partner(n):
        m = lax.div(n, NX)
        far = jnp.where(lax.rem(m, 2) == 1, 4 - lax.div(m + 1, 2), 4 + lax.div(m, 2))
        return (lax.rem(x + 3 - lax.rem(n, NX), NX), lax.rem(y + far, NY))

    label = jnp.bitwise_xor(jnp.bitwise_xor(irreps[v], irreps[zl]), irreps[0])
    lane = lax.broadcasted_iota(jnp.int32, (8, PIECE), 1) & 255
    kept = jnp.zeros((8, PIECE), jnp.float32)
    for n in range(DW // VBLK):
        same = jnp.where(irreps[y * (DW // VBLK) + n] == label, 1.0, 0.0)
        kept = jnp.where(lane >> 4 == n, same, kept)
    v_own[...] = jnp.zeros_like(v_own)
    v_load.wait()
    for b in range(4):
        for c in range(CW):
            part = v_raw[:, c, b, :].astype(jnp.float32) * kept[0:1, :DW]
            v_own[b * 16 : b * 16 + 16, c * 256 : c * 256 + DW] = part.astype(jnp.bfloat16)

    m = lax.broadcasted_iota(jnp.int32, (1024, 128), 0)
    n = lax.broadcasted_iota(jnp.int32, (1024, 128), 1)
    hit = jnp.logical_and(m >> 7 == n >> 4, (m & 127) == (n & 15) + v * 16)
    pull[...] = jnp.where(hit, 1.0, 0.0).astype(jnp.bfloat16)
    for load in t_loads:
        load.wait()
    wide = jnp.concatenate(
        [
            jnp.concatenate([t_all[q, :, c * NV : c * NV + 128] for q in range(8)], axis=1)
            for c in range(CW)
        ],
        axis=0,
    )
    a_own[...] = dot(wide, pull[...]).astype(jnp.bfloat16).reshape(CW, 16, 128)
    pl.semaphore_wait(barrier, 3 + 2 + 15)

    names = {}
    sends = []

    def sem(*name):
        return names.setdefault(name, len(names))

    def hop(src, dst, where, *name):
        n = sem(*name)
        return remote(src, dst, ssem.at[n], rsem.at[n], where)

    def go(copy):
        copy.start()
        sends.append(copy)

    t_block = (1, 2)

    def t_rows(block, u):
        return t_all.at[pl.ds(block * 8 + k * 4 + u, 1)]

    def t_copy(d, i):
        u = 3 * d + (1 - 2 * d) * i
        return hop(t_rows(0, u), t_rows(t_block[d], u), dev(x, y, zn[d], k), "t", d, i)

    def t_forward(d, i):
        u = 3 * d + (1 - 2 * d) * i
        return hop(t_rows(t_block[d], u), t_rows(3, u), dev(x, y, zn[d], k), "tf", d, i)

    def t_sibling(block, u):
        return hop(t_rows(block, u), t_rows(block, u), dev(x, y, z, 1 - k), "ts", block, u)

    def t_start(i):
        for d in range(2):
            go(t_copy(d, i))

    def t_step(i):
        for d in range(2):
            t_copy(d, i).wait_recv()
            if i < 2:
                go(t_forward(d, i))
            go(t_sibling(t_block[d], 3 * d + (1 - 2 * d) * i))

    def t_last(i):
        for d in range(2):
            t_forward(d, i).wait_recv()
            go(t_sibling(3, 3 * d + (1 - 2 * d) * i))

    def slab_place(block):
        rows = pl.ds(pl.multiple_of(y * 16, 16), 16)
        return a_mat.at[:, rows, pl.ds(pl.multiple_of(block * 128, 128), 128)]

    slab_rows = a_mat.at[:, pl.ds(pl.multiple_of(y * 16, 16), 16), :]

    def slab_y(d, s):
        slot = lax.rem(y + (NY - s if d == 0 else s), NY)
        part = a_mat.at[:, pl.ds(pl.multiple_of(slot * 16, 16), 16), :]
        return hop(part, part, dev(x, ys[d], z, k), "b", d, s)

    def v0_y(d, s):
        slot = s0.at[lax.rem(y + (NY - s if d == 0 else s), NY)]
        return hop(slot, slot, dev(x, ys[d], z, k), "v0y", d, s)

    def v0_rows(slot, part):
        return v_all.at[pl.ds(pl.multiple_of(slot * 64 + part * 16, 16), 16)]

    def v0_x(d, part):
        rows = v0_rows(x, part)
        return hop(rows, rows, dev(xs[d], y, z, k), "v0x", d, part)

    def v0_f(d):
        rows = v0_rows(xs[1 - d], d)
        return hop(rows, rows, dev(xs[d], y, z, k), "v0f", d)

    def v1_x(n):
        slot = x1.at[x]
        return hop(slot, slot, dev(lax.rem(x + n, NX), y, z, k), "v1x", n)

    def v1_y(d, s, e):
        lanes = pl.ds(1408 * e, 1408 - 128 * e)
        slot = s1.at[lax.rem(y + (NY - s if d == 0 else s), NY), :, lanes]
        return hop(slot, slot, dev(x, ys[d], z, k), "v1y", d, s, e)

    there = pick(v * 4 + zl, PLACE_OF)
    moves = there != z * 2 + k
    go_there = dev(x, y, lax.div(there, 2), lax.rem(there, 2))
    raw = [
        (v_own.at[pl.ds(0, 32)], s0.at[y], sem("r", 0)),
        (v_own.at[pl.ds(32, 32)], x1.at[x], sem("r", 1)),
    ]

    @pl.when(moves)
    def _():
        for src, dst, n in raw:
            remote(src, dst, ssem.at[n], rsem.at[n], go_there).start()

    @pl.when(jnp.logical_not(moves))
    def _():
        for src, dst, n in raw:
            pltpu.make_async_copy(src, dst, rsem.at[n]).start()

    for b in range(4):
        at = pick(v * 4 + b, PLACE_OF)
        az, ak = lax.div(at, 2), lax.rem(at, 2)
        above = lax.rem(zl - lax.rem(az, NZL) + NZL, NZL)
        block = jnp.where(above == 0, 0, jnp.where(above == 3, 1, above + 1))
        mine = at == z * 2 + k

        @pl.when(mine)
        def _():
            pltpu.make_async_copy(a_own, slab_place(0), a_recv).start()

        @pl.when(jnp.logical_not(mine))
        def _():
            remote(a_own, slab_place(block), a_send, a_recv, dev(x, y, az, ak)).start()

    for src, dst, n in raw:
        pltpu.make_async_copy(src, dst, rsem.at[n]).wait()
        if n == raw[0][2]:
            go(v0_y(0, 0))
            go(v0_y(1, 0))
    for n in range(1, NX):
        go(v1_x(n))
    t_start(0)
    t_start(1)

    def v0_step(s):
        v0_y(0, s).wait_recv()
        if s < 3:
            go(v0_y(0, s + 1))
            v0_y(1, s).wait_recv()
        if s < 2:
            go(v0_y(1, s + 1))

    def v1_step(s):
        for e in range(2):
            for d in range(2):
                if s == 3 and d != e:
                    continue
                v1_y(d, s, e).wait_recv()
                if s < 2 or (s == 2 and d == e):
                    go(v1_y(d, s + 1, e))

    def slab_step(s):
        for d in range(2):
            if s == 3 and d == 1:
                continue
            slab_y(d, s).wait_recv()
            if s < 3 - d:
                go(slab_y(d, s + 1))

    def join(source, rows, half):
        for c in range(CW):
            joined = jnp.concatenate([source(half * 4 + q, c) for q in range(4)], axis=1)
            v_all[rows, pl.ds(pl.multiple_of(c * NV + half * 896, 128), 896)] = joined

    def join0(half):
        rows = pl.ds(pl.multiple_of(x * 64, 32), 32)
        join(lambda q, c: s0[q, :, c * 256 : c * 256 + DW], rows, half)

    def join1(half):
        for slot in range(NX):
            first_lane = slot * CW * DW
            join(
                lambda q, c: s1[q, :, first_lane + c * DW : first_lane + c * DW + DW],
                pl.ds(slot * 64 + 32, 32),
                half,
            )

    near_half = lax.div(y, 4)

    def ladder(pair, half):
        for c in range(CW):
            ks = pl.ds(pl.multiple_of(c * NV + half * 896, 128), 896)
            both = dot(t_all[pl.ds(pair * 16, 16), :, ks].reshape(256, 896), v_all[:, ks], NT)
            for h in range(2):
                acc[h, pl.ds(pair * 256, 256), :] += both[:, h * 128 : h * 128 + 128]

    v0_step(0)
    for n in range(1, NX):
        v1_x(n).wait_recv()
    s1[y] = jnp.concatenate(
        [x1[slot, :, c * 256 : c * 256 + DW] for slot in range(NX) for c in range(CW)], axis=1
    )
    for e in range(2):
        go(v1_y(0, 0, e))
        go(v1_y(1, 0, e))
    v0_step(1)
    pltpu.make_async_copy(slab_rows, slab_rows, a_recv).wait()
    go(slab_y(0, 0))
    go(slab_y(1, 0))
    v0_step(2)
    t_step(0)
    t_start(2)
    v1_step(0)
    t_step(1)
    t_start(3)
    v0_step(3)
    for half in range(2):
        join0(half)
    go(v0_x(0, 0))
    go(v0_x(1, 1))
    go(v0_x(0, 1))
    go(v0_x(1, 0))
    slab_step(0)
    v1_step(1)
    slab_step(1)
    v0_x(0, 0).wait_recv()
    go(v0_f(0))
    v0_x(1, 1).wait_recv()
    go(v0_f(1))
    slab_step(2)
    t_step(2)
    v1_step(2)
    slab_step(3)
    w_load.wait()
    zmat = None
    for c in range(CW):
        rows = w_own[:, c, pl.ds(pl.multiple_of(blk_b * 16, 16), 16), :].reshape(256, NO)
        part = dot(rows, a_mat[c])
        zmat = part if zmat is None else zmat + part
    for block in range(4):
        zs[block, 0:256, :] = zmat[:, block * 128 : block * 128 + 128]
    chunk = lax.broadcasted_iota(jnp.int32, (16, 128), 1) >> 4

    def crossed(block, carry):
        for h in range(2):
            outs = [jnp.zeros((16, 128), jnp.float32)] * 8
            for b in range(8):
                part = zs[block, pl.ds(h * 8 + b, 16, stride=16), :]
                for q in range(8):
                    moved = pltpu.roll(part, (b - q) % 8 * 16, 1) if b != q else part
                    outs[q] = jnp.where(chunk == b, -moved, outs[q])
            for q in range(8):
                acc[h, pl.ds(pl.multiple_of(block * 128 + q * 16, 16), 16), :] = outs[q]
        return carry

    lax.fori_loop(0, 4, crossed, 0)

    t_step(3)
    t_last(0)
    v0_x(0, 1).wait_recv()
    v0_x(1, 0).wait_recv()
    for d in range(2):
        v0_f(d).wait_recv()
    join1(near_half)
    for u in range(4):
        t_sibling(1, u).wait_recv()
    ladder(0, near_half)
    v1_step(3)
    join1(1 - near_half)
    def near(n):
        return lax.rem(zl + ABOVE[n], NZL)

    def tile_row(si, sj, h):
        return (si // 2 * 2 + sj // 2) * 8 + (si % 2 * 2 + sj % 2) * 2 + h

    def fill(pair, half):
        for si in (2 * pair, 2 * pair + 1):
            for sj in (2 * half, 2 * half + 1):
                for xj in range(4):
                    for h in range(2):
                        mail[pl.ds(xj * 256 + tile_row(si, sj, h), 8, stride=32), :] = acc[
                            h, pl.ds(si * 128 + near(sj) * 4 + xj, 8, stride=16), :
                        ]

    def post(part, start, rows):
        def send_mail(n, carry):
            px, py = partner(n)
            src = mail.at[pl.ds(pl.multiple_of((px * 8 + py) * 32 + start, 8), rows)]
            dst = rec.at[pl.ds(pl.multiple_of((x * 8 + y) * 32 + start, 8), rows)]
            remote(src, dst, m_send.at[part], m_recv.at[part], dev(px, py, z, twin)).start()
            return carry

        lax.fori_loop(0, 32 - first, send_mail, 0)

        @pl.when(diag)
        def _():
            here = pl.ds(pl.multiple_of((x * 8 + y) * 32 + start, 8), rows)
            pltpu.make_async_copy(mail.at[here], rec.at[here], m_recv.at[part]).start()

    ladder(0, 1 - near_half)
    fill(0, 0)
    fill(0, 1)
    post(0, 0, 16)
    t_last(1)
    for block in (2, 3):
        for u in range(4):
            t_sibling(block, u).wait_recv()
    for half in range(2):
        ladder(1, half)
    fill(1, 0)
    post(1, 16, 8)
    fill(1, 1)
    post(2, 24, 8)

    m = lax.broadcasted_iota(jnp.int32, (256, 256), 0)
    n = lax.broadcasted_iota(jnp.int32, (256, 256), 1)
    hit = jnp.logical_and(m >> 4 == (n & 15), (m & 15) == n >> 4)
    swap[...] = jnp.where(hit, 1.0, 0.0).astype(jnp.bfloat16)
    lane = lax.broadcasted_iota(jnp.int32, (16, 256), 1)
    line = lax.broadcasted_iota(jnp.int32, (16, 256), 0)
    e_j = jnp.zeros((16, 256), jnp.float32)
    e_a = jnp.zeros((16, 256), jnp.float32)
    e_b = jnp.zeros((16, 256), jnp.float32)
    for n in range(16):
        e_j = jnp.where(line == n, occ[y * 16 + n], e_j)
        e_a = jnp.where(lane >> 4 == n, vir[blk_a * 16 + n], e_a)
        e_b = jnp.where((lane & 15) == n, vir[blk_b * 16 + n], e_b)
    for block in range(4):
        for q in range(8):
            e_i = occ[q * 16 + lax.rem(zl + ABOVE[block], NZL) * 4 + x]
            denom[block * 128 + q * 16 : block * 128 + q * 16 + 16, :] = ((e_i + e_j) - e_a) - e_b
    m = lax.broadcasted_iota(jnp.int32, (512, 512), 0)
    n = lax.broadcasted_iota(jnp.int32, (512, 512), 1)
    hit = jnp.logical_and((m >> 4 & 7) == n >> 6, m >> 7 == (n >> 4 & 3))
    hit = jnp.logical_and(hit, (m & 15) == (n & 15))
    order[...] = jnp.where(hit, 1.0, 0.0).astype(jnp.bfloat16)

    owner_z = lax.div(blk_a, 2) * NZL
    owner_k = lax.rem(blk_a, 2)
    for block in range(4):
        rows = pl.ds(block * 128, 128)
        turned = None
        for h in range(2):
            part = acc[h, rows, :]
            hi = part.astype(jnp.bfloat16)
            rest = part - hi.astype(jnp.float32)
            mid = rest.astype(jnp.bfloat16)
            low = (rest - mid.astype(jnp.float32)).astype(jnp.bfloat16)
            matrix = swap[h * 128 : h * 128 + 128, :]
            term = dot(hi, matrix) + (dot(mid, matrix) + dot(low, matrix))
            turned = term if turned is None else turned + term
        for h in range(2):
            own_x[h, rows, :] = turned[:, h * 128 : h * 128 + 128]

    def arrived(part, count):
        some = rec.at[pl.ds(0, count)]
        pltpu.make_async_copy(some, some, m_recv.at[part]).wait()

    def take(pair, half):
        for si in (2 * pair, 2 * pair + 1):
            for sj in (2 * half, 2 * half + 1):
                for xj in range(4):
                    for h in range(2):
                        rows = pl.ds(sj * 128 + near(si) * 4 + xj, 8, stride=16)
                        own_x[h, rows, :] += rec[pl.ds(xj * 256 + tile_row(si, sj, h), 8, stride=32), :]

    arrived(0, 512)
    take(0, 0)
    take(0, 1)
    for half in range(2):
        arrived(1 + half, 256)
        take(1, half)
        for sj in (2 * half, 2 * half + 1):
            rows = pl.ds(sj * 128, 128)
            for h in range(2):
                lanes = pl.ds(h * 128, 128)
                sbuf[rows, lanes] = (own_x[h, rows, :] / denom[rows, lanes]).astype(jnp.bfloat16)
            target = owner_z + near(sj)
            n = sem("d", sj)
            if sj == 0:

                @pl.when(own)
                def _():
                    pltpu.make_async_copy(sbuf.at[rows], d_all.at[blk_b], d_recv.at[blk_b]).start()

                @pl.when(jnp.logical_not(own))
                def _():
                    remote(sbuf.at[rows], d_all.at[blk_b], ssem.at[n], d_recv.at[blk_b], dev(x, y, target, owner_k)).start()
            else:
                go(remote(sbuf.at[rows], d_all.at[blk_b], ssem.at[n], d_recv.at[blk_b], dev(x, y, target, owner_k)))

    parts = [None, None]
    for b in range(4):
        pltpu.make_async_copy(d_all.at[b], d_all.at[b], d_recv.at[b]).wait()
        for h in range(2):
            term = dot(d_all[b, :, h * 128 : h * 128 + 128], order[b * 128 : b * 128 + 128, :])
            parts[h] = term if b == 0 else parts[h] + term
    for h in range(2):
        out_ref[:, h * 512 : h * 512 + 512] = parts[h].astype(jnp.bfloat16)

    for copy in sends:
        copy.wait_send()

    @pl.when(moves)
    def _():
        for src, dst, n in raw:
            pltpu.make_async_copy(src, src, ssem.at[n]).wait()

    @pl.when(jnp.logical_not(own))
    def _():
        some = sbuf.at[pl.ds(0, 128)]
        pltpu.make_async_copy(some, some, ssem.at[sem("d", 0)]).wait()

    three = a_mat.at[:, pl.ds(0, 16), pl.ds(0, 384)]

    @pl.when(own)
    def _():
        pltpu.make_async_copy(three, three, a_send).wait()

    @pl.when(jnp.logical_not(own))
    def _():
        pltpu.make_async_copy(slab_rows, slab_rows, a_send).wait()

    for part, rows in ((0, 16), (1, 8), (2, 8)):

        @pl.when(diag)
        def _():
            some = rec.at[pl.ds(0, 31 * rows)]
            pltpu.make_async_copy(some, some, m_send.at[part]).wait()

        @pl.when(jnp.logical_not(diag))
        def _():
            some = rec.at[pl.ds(0, 32 * rows)]
            pltpu.make_async_copy(some, some, m_send.at[part]).wait()


def call(t, vv, w, irreps, occ, vir):
    bf, f32 = jnp.bfloat16, jnp.float32
    vm = pl.BlockSpec(memory_space=pltpu.VMEM)
    smem = pl.BlockSpec(memory_space=pltpu.SMEM)
    anywhere = pl.BlockSpec(memory_space=pl.ANY)
    dma = pltpu.SemaphoreType.DMA
    return pl.pallas_call(
        kernel,
        out_shape=jax.ShapeDtypeStruct((NO, 1024), bf),
        in_specs=[anywhere, anywhere, anywhere, smem, smem, smem],
        out_specs=vm,
        scratch_shapes=[
            pltpu.VMEM((32, 16, KK), bf),
            pltpu.VMEM((NY, 32, PIECE), bf),
            pltpu.VMEM((NX, 32, PIECE), bf),
            pltpu.VMEM((NY, 32, NX * CW * DW), bf),
            pltpu.VMEM((256, KK), bf),
            pltpu.VMEM((CW, NO, 512), bf),
            pltpu.VMEM((4, 288, 128), f32),
            pltpu.VMEM((2, 528, 128), f32),
            pltpu.VMEM((2, 528, 128), f32),
            pltpu.VMEM((512, 512), bf),
            pltpu.VMEM((256, 256), bf),
            pltpu.VMEM((1024, 128), bf),
            pltpu.VMEM((CW, 16, 128), bf),
            pltpu.VMEM((16, CW, 4, DW), bf),
            pltpu.VMEM((64, PIECE), bf),
            pltpu.VMEM((16, CW, SA, NO), bf),
            pltpu.VMEM((512, 256), f32),
            pltpu.VMEM((1056, 128), f32),
            pltpu.VMEM((1056, 128), f32),
            pltpu.VMEM((512, 256), bf),
            pltpu.VMEM((4, 128, 256), bf),
            dma((96,)), dma((96,)), dma((5,)), dma, dma, dma((3,)), dma((3,)), dma((4,)),
        ],
        compiler_params=pltpu.CompilerParams(
            collective_id=0, has_side_effects=True, vmem_limit_bytes=64 * 1024 * 1024
        ),
        cost_estimate=pl.CostEstimate(flops=2 * 512 * 256 * KK, bytes_accessed=20_000_000, transcendentals=0),
    )(t, vv, w, irreps, occ, vir)


def local(amplitudes, integrals, hole_integrals, irreps, occ_energy, vir_energy):
    t = jnp.transpose(amplitudes.reshape(8, 16, CW, NV), (0, 2, 1, 3))
    vv = jnp.transpose(integrals, (0, 2, 1, 3))
    w = jnp.transpose(hole_integrals.reshape(NO, 16, CW, SA), (1, 2, 3, 0))
    out = call(t, vv, w, irreps, occ_energy, vir_energy)
    return out.reshape(8, 1, 1, 1, 16, 16, SA)


def solution(mesh):
    in_specs = (
        P(None, "row", None, "col", None, None, None),
        P("vir", "row", None, "col"),
        P(None, None, "col", None, None, None),
        P(),
        P(),
        P(),
    )
    out_specs = P(None, "row", None, "col", None, "vir", None)
    return jax.shard_map(local, mesh=mesh, in_specs=in_specs, out_specs=out_specs, check_vma=False)
```
